128 devices in a mesh: gx: 4 (over z), gy: 4 (over y), gz: 8 (over x, core).
Axes of the slice: x: 4, y: 4, z: 4, core: 2. Of those that a mesh axis runs over, the one named last changes fastest.
Arguments:
- offsets: float32 [4, 4, 8, 3, 4096], P('gx', 'gy', 'gz'), may hold values from -0.25 to 0.25
- burgers: float32 [4, 4, 8, 3, 4096], P('gx', 'gy', 'gz'), may hold values from -4 to 4
- segvec: float32 [4, 4, 8, 3, 4096], P('gx', 'gy', 'gz'), may hold values from -0.4 to 0.4
- block_cell: int32 [4, 4, 8, 16], P('gx', 'gy', 'gz'), may hold values from 0 to 7, as said below
- tree_level: int32 [128], P(('gx', 'gy', 'gz')), may hold values 0 or 1
- pair_count: int32 [128], P(('gx', 'gy', 'gz')), may hold values from 1 to 48, 2048 in all
- pair_list: int32 [4, 4, 8, 3, 48], P('gx', 'gy', 'gz'), may hold values from 0 to 26, as said below
Outputs:
- forces: float32 [4, 4, 8, 3, 4096], P('gx', 'gy', 'gz')
The draws below stay inside these ranges and needn't reach their ends.
Inputs may be any that keep to these rules, and one draw needn't show every extreme that they name: block_cell names a subcell of the block's own domain; the first min(16, 8) blocks of a domain lie in different subcells, so with 16 >= 8 every subcell holds a block. The first 48 entries hold pair_count[d] live pairs of domain d; the rest are padding. `pair_list`: row 0 and row 2 are block numbers below 16, row 1 a neighbour slot below 27; slot 13 is the domain itself and then the two blocks differ; the two blocks of an entry lie in touching subcells: along each dimension their subcell centres, the neighbour offset included, differ by at most 0.5; a pair may be listed more than once.
All inputs are finite; a program needn't handle non-finite values. No bound on the sum of `tree_level` or of `pair_count` on one device may be relied on, other than what follows from the above.
Results may differ from the reference program's by a relative error of at most 0.0003.
Values sent between devices are 32-bit elements; how exact they have to be, the bound alone decides.
No kernel may reach another device: no remote copies, remote signals or barrier semaphores. Data moves between devices by JAX's collectives and lax.ppermute only.
A program may use at most 64 MiB of HBM per device.

```python
import math
import jax
import jax.numpy as jnp
import numpy as np
from jax import lax

BLOCK = 256
BLK_DEV = 16
SEG_DEV = 4096
PAIR_CAP = 48
CELLS_X = 4
CELLS_Y = 4
CELLS_Z = 8
DOMAINS = 128


def shared_cells(key):
    key = jax.random.fold_in(key, 5)
    order_key, extra_key = jax.random.split(key, 2)
    domains = CELLS_X * CELLS_Y * CELLS_Z
    order_keys = jax.random.split(order_key, domains)
    orders = jax.vmap(lambda single: jax.random.permutation(single, 8))(order_keys)
    extra = jax.random.randint(extra_key, (domains, BLK_DEV), 0, 8)
    index = jnp.arange(BLK_DEV, dtype=jnp.int32)
    cells = jnp.where(index[None, :] < 8, orders[:, jnp.minimum(index, 7)], extra)
    return cells.reshape(CELLS_X, CELLS_Y, CELLS_Z, BLK_DEV).astype(jnp.int32)


def draw_block_cell(key, part):
    cells = shared_cells(key)
    return cells


def draw_pair_list(key, part):
    cells = shared_cells(key)
    key = jax.random.fold_in(key, 11)
    first_key, move_key, pick_key = jax.random.split(key, 3)
    shape = (CELLS_X, CELLS_Y, CELLS_Z, PAIR_CAP)
    first = jax.random.randint(first_key, shape, 0, BLK_DEV).astype(jnp.int32)
    own_cell = jnp.take_along_axis(cells, first, axis=3)
    bits = [own_cell // divider % 2 for divider in (4, 2, 1)]
    moving = jax.random.randint(move_key, (3,) + shape, 0, 2).astype(jnp.int32)
    steps = [moving[member] * (2 * bits[member] - 1) for member in range(3)]
    place_x = jnp.arange(CELLS_X, dtype=jnp.int32)[:, None, None, None]
    place_y = jnp.arange(CELLS_Y, dtype=jnp.int32)[None, :, None, None]
    place_z = jnp.arange(CELLS_Z, dtype=jnp.int32)[None, None, :, None]
    near_x = (place_x + steps[0]) % CELLS_X
    near_y = (place_y + steps[1]) % CELLS_Y
    near_z = (place_z + steps[2]) % CELLS_Z
    near_cells = cells[near_x, near_y, near_z]
    fitting = jnp.ones(shape + (BLK_DEV,), dtype=bool)
    for member, divider in enumerate((4, 2, 1)):
        near_bits = near_cells // divider % 2
        fitting = fitting & ((moving[member] == 0)[..., None] | (near_bits == (1 - bits[member])[..., None]))
    staying = moving[0] + moving[1] + moving[2] == 0
    index = jnp.arange(BLK_DEV, dtype=jnp.int32)
    fitting = fitting & ~(staying[..., None] & (index == first[..., None]))
    noise = jax.random.randint(pick_key, shape + (BLK_DEV,), 0, 1024).astype(jnp.int32)
    score = fitting.astype(jnp.int32) * (1024 * BLK_DEV) + noise * BLK_DEV + index
    second = jnp.argmax(score, axis=-1).astype(jnp.int32)
    found = jnp.any(fitting, axis=-1)
    slot = (steps[0] + 1) * 9 + (steps[1] + 1) * 3 + steps[2] + 1
    slot = jnp.where(found, slot, 13)
    second = jnp.where(found, second, (first + 1) % BLK_DEV)
    return jnp.stack([first, slot, second], axis=3).astype(jnp.int32)


def plant(values, stream_key, least, high):
    shape = values.shape
    index_at = [jax.random.randint(jax.random.fold_in(stream_key, axis), (), 0, shape[axis]) for axis in range(len(shape))]
    values = values.at[tuple(index_at)].set(least)
    longest = shape.index(max(shape))
    index_at[longest] = (index_at[longest] + 1) % shape[longest]
    return values.at[tuple(index_at)].set(high)


def block_scale(rng, shape, pieces, least, top_value):
    def one(dim, parts):
        steps = jax.random.uniform(jax.random.fold_in(jax.random.fold_in(rng, 6), dim), (parts,), jnp.float32, least / len(pieces), top_value / len(pieces))
        return jnp.repeat(jnp.exp(steps), shape[dim] // parts).reshape((-1,) + (1,) * (len(shape) - dim - 1))

    gain = one(*pieces[0])
    for cut in pieces[1:]:
        gain = gain * one(*cut)
    return gain


def profile(number_of, total, most, skew):
    loads = [(1 << 20) // math.isqrt(rank ** skew) + 1 for rank in range(2, number_of + 1)]
    spare, given = total - most - (number_of - 1), [1] * (number_of - 1)
    while spare > 0:
        movable = [i for i in range(number_of - 1) if given[i] < most]
        whole, left = sum([loads[i] for i in movable]), spare
        for i in movable:
            more = min(most - given[i], max(1, left * loads[i] // whole), spare)
            given[i] = given[i] + more
            spare = spare - more
    return np.array([most] + given)


def uneven_parts(own_key, number_of, total, limit, skew):
    if number_of == 2:
        one = jax.random.randint(own_key, (), max(1, total - limit), min(limit, total - 1) + 1)
        return jnp.stack([one, total - one])
    tallies = jnp.asarray(profile(number_of, total, limit, skew), jnp.int32)
    pairs = (number_of - 1) // 2
    source_of, taker = tallies[1:1 + 2 * pairs:2], tallies[2:2 + 2 * pairs:2]
    slack = jnp.minimum(source_of - 1, limit - taker)
    passed = jax.random.randint(jax.random.fold_in(own_key, 1), (pairs,), 0, 1 << 20) % (slack + 1)
    tallies = tallies.at[1:1 + 2 * pairs:2].set(source_of - passed).at[2:2 + 2 * pairs:2].set(taker + passed)
    return tallies[jax.random.permutation(jax.random.fold_in(own_key, 2), number_of)]


def scatter_about(stream_key, extent, deviation, most, cuts=(), kind=jnp.bfloat16):
    array = jax.random.normal(stream_key, extent, jnp.float32) * deviation
    if len(cuts) > 0:
        array = block_scale(stream_key, extent, cuts, -0.22, 0.18) * array
    return jnp.clip(array, min=-most, max=most).astype(kind)


def setup_inputs(seed: int = 0) -> dict:
    key_list = jax.random.split(jax.random.key(seed), 8)
    return {
        "offsets": jnp.clip(jax.random.uniform(key_list[0], (CELLS_X, CELLS_Y, CELLS_Z, 3, SEG_DEV), jnp.float32, -0.25, 0.25) * block_scale(key_list[0], (CELLS_X, CELLS_Y, CELLS_Z, 3, SEG_DEV), ((0, 4), (1, 4), (2, 8)), -0.4, 0.0), -0.25, 0.25),
        "burgers": scatter_about(key_list[1], (CELLS_X, CELLS_Y, CELLS_Z, 3, SEG_DEV), 1.0, 4.0, ((0, 4), (1, 4), (2, 8)), jnp.float32),
        "segvec": scatter_about(key_list[2], (CELLS_X, CELLS_Y, CELLS_Z, 3, SEG_DEV), 0.1, 0.4, ((0, 4), (1, 4), (2, 8)), jnp.float32),
        "block_cell": draw_block_cell(jax.random.fold_in(key_list[7], 71), 0),
        "tree_level": plant((jax.random.randint(key_list[4], (DOMAINS,), 0, 2) < 1).astype(jnp.int32), jax.random.fold_in(key_list[4], 1), 0, 1),
        "pair_count": uneven_parts(key_list[5], DOMAINS, DOMAINS * BLK_DEV, PAIR_CAP, 2).astype(jnp.int32),
        "pair_list": draw_pair_list(jax.random.fold_in(key_list[7], 71), 0),
    }


core_square = 0.04

def subcell_centre(labels):
    return [(labels // divider % 2).astype(jnp.float32) * 0.5 + 0.25 for divider in (4, 2, 1)]

def moment_of(burger, segment):
    return [burger[0] * segment[0], burger[1] * segment[1], burger[2] * segment[2], 0.5 * (burger[1] * segment[2] + burger[2] * segment[1]), 0.5 * (burger[0] * segment[2] + burger[2] * segment[0]), 0.5 * (burger[0] * segment[1] + burger[1] * segment[0])]

def stress_of(moment, displace, cubed, fifths):
    xx_part, yy_part, zz_part, yz_part, xz_part, xy_part = moment
    along_x = xx_part * displace[0] + xy_part * displace[1] + xz_part * displace[2]
    along_y = xy_part * displace[0] + yy_part * displace[1] + yz_part * displace[2]
    along_z = xz_part * displace[0] + yz_part * displace[1] + zz_part * displace[2]
    weight = 3.0 * fifths
    return [xx_part * cubed - weight * along_x * displace[0], yy_part * cubed - weight * along_y * displace[1], zz_part * cubed - weight * along_z * displace[2], yz_part * cubed - 0.5 * weight * (along_y * displace[2] + along_z * displace[1]), xz_part * cubed - 0.5 * weight * (along_x * displace[2] + along_z * displace[0]), xy_part * cubed - 0.5 * weight * (along_x * displace[1] + along_y * displace[0])]

def force_of(stress, burger, segment):
    xx_part, yy_part, zz_part, yz_part, xz_part, xy_part = stress
    push_x = xx_part * burger[0] + xy_part * burger[1] + xz_part * burger[2]
    push_y = xy_part * burger[0] + yy_part * burger[1] + yz_part * burger[2]
    push_z = xz_part * burger[0] + yz_part * burger[1] + zz_part * burger[2]
    return [push_y * segment[2] - push_z * segment[1], push_z * segment[0] - push_x * segment[2], push_x * segment[1] - push_y * segment[0]]

def powers(displace):
    distance = displace[0] * displace[0] + displace[1] * displace[1] + displace[2] * displace[2] + core_square
    inverse = lax.rsqrt(distance)
    cubed = inverse * inverse * inverse
    return (cubed, cubed * inverse * inverse)

def pair_forces(mine, other, shifts):
    displace = [mine[:, member, :, None] - other[:, member, None, :] - shifts[:, member, None, None] for member in range(3)]
    cubed, fifths = powers(displace)
    source = moment_of([other[:, 3 + member, None, :] for member in range(3)], [other[:, 6 + member, None, :] for member in range(3)])
    on_mine = [lax.optimization_barrier(jnp.sum(term, axis=2)) for term in stress_of(source, displace, cubed, fifths)]
    backward = moment_of([mine[:, 3 + member, :, None] for member in range(3)], [mine[:, 6 + member, :, None] for member in range(3)])
    on_other = [lax.optimization_barrier(jnp.sum(term, axis=1)) for term in stress_of(backward, displace, cubed, fifths)]
    first = force_of(on_mine, [mine[:, 3 + member] for member in range(3)], [mine[:, 6 + member] for member in range(3)])
    second = force_of(on_other, [other[:, 3 + member] for member in range(3)], [other[:, 6 + member] for member in range(3)])
    return (jnp.stack(first, axis=1), jnp.stack(second, axis=1))

def far_field(target, source, moment):
    displace = [target[member][:, None] - source[member][None, :] for member in range(3)]
    cubed, fifths = powers(displace)
    stress = stress_of([moment[member][None, :] for member in range(6)], displace, cubed, fifths)
    return jnp.stack([lax.optimization_barrier(jnp.sum(term, axis=1)) for term in stress])

def signed_step(difference, count):
    wrapped = difference % count
    return jnp.where(wrapped > count // 2, wrapped - count, wrapped)

def far_mask(steps):
    largest = jnp.maximum(jnp.maximum(jnp.abs(steps[0]), jnp.abs(steps[1])), jnp.abs(steps[2]))
    return (largest > 1).astype(jnp.float32)

def reference(offsets, burgers, segvec, block_cell, tree_level, pair_count, pair_list):
    domains = CELLS_X * CELLS_Y * CELLS_Z
    extents = [CELLS_X, CELLS_Y, CELLS_Z]
    labels = jnp.repeat(block_cell.reshape(domains, BLK_DEV), BLOCK, axis=1)
    position = jnp.stack(subcell_centre(labels), axis=1) + offsets.reshape(domains, 3, SEG_DEV)
    burger = burgers.reshape(domains, 3, SEG_DEV)
    segment = segvec.reshape(domains, 3, SEG_DEV)
    state = jnp.concatenate([position, burger, segment], axis=1).reshape(domains, 9, BLK_DEV, BLOCK)
    pairs = pair_list.reshape(domains, 3, PAIR_CAP)

    def coords(ident):
        return [ident // (CELLS_Y * CELLS_Z), ident // CELLS_Z % CELLS_Y, ident % CELLS_Z]

    def visit(totals, flat):
        owner = flat // PAIR_CAP
        which = flat % PAIR_CAP
        first = pairs[owner, 0, which]
        slot = pairs[owner, 1, which]
        second = pairs[owner, 2, which]
        steps = [slot // 9 - 1, slot // 3 % 3 - 1, slot % 3 - 1]
        place = coords(owner)
        moved = [(place[member] + steps[member]) % extents[member] for member in range(3)]
        neighbour = (moved[0] * CELLS_Y + moved[1]) * CELLS_Z + moved[2]
        shifts = jnp.stack(steps).astype(jnp.float32)[None]
        near_first, near_second = pair_forces(state[owner, :, first][None], state[neighbour, :, second][None], shifts)
        live = (which < pair_count[owner]).astype(jnp.float32)
        totals = totals.at[owner, :, first].add(live * near_first[0])
        totals = totals.at[neighbour, :, second].add(live * near_second[0])
        return (totals, None)
    start = jnp.zeros((domains, 3, BLK_DEV, BLOCK), jnp.float32)
    near, _ = lax.scan(visit, start, jnp.arange(domains * PAIR_CAP, dtype=jnp.int32))
    onehot = (labels[:, None, :] == jnp.arange(8, dtype=jnp.int32)[None, :, None]).astype(jnp.float32)
    moment = jnp.stack(moment_of([burger[:, member] for member in range(3)], [segment[:, member] for member in range(3)]), axis=1)
    sub_moment = jnp.einsum('dcs,dks->dck', moment, onehot, precision=lax.Precision.HIGHEST)
    table = jnp.stack(subcell_centre(jnp.arange(8, dtype=jnp.int32)))
    source_pos = jnp.where(tree_level[:, None, None] == 1, table[None], 0.5)
    idents = jnp.arange(domains, dtype=jnp.int32)
    other_place = coords(idents)

    def target(ident):
        place = coords(ident)
        steps = [signed_step(other_place[member] - place[member], extents[member]) for member in range(3)]
        distant = far_mask(steps)
        moved = source_pos + jnp.stack(steps, axis=1).astype(jnp.float32)[:, :, None]
        masked = sub_moment * distant[:, None, None]
        return far_field(table, jnp.moveaxis(moved, 1, 0).reshape(3, domains * 8), jnp.moveaxis(masked, 1, 0).reshape(6, domains * 8))
    far_stress = lax.map(target, idents)
    seg_stress = jnp.einsum('dck,dks->dcs', far_stress, onehot, precision=lax.Precision.HIGHEST)
    far_force = jnp.stack(force_of([seg_stress[:, member] for member in range(6)], [burger[:, member] for member in range(3)], [segment[:, member] for member in range(3)]), axis=1)
    total = near.reshape(domains, 3, SEG_DEV) + far_force
    return total.reshape(CELLS_X, CELLS_Y, CELLS_Z, 3, SEG_DEV)
```

```python
import functools

import jax
import jax.numpy as jnp
from jax import lax
from jax.experimental import pallas as pl
from jax.experimental.pallas import tpu as pltpu
from jax.sharding import PartitionSpec as P

F32, BF16, I32 = jnp.float32, jnp.bfloat16, jnp.int32
CORE = 0.04
WIDTH = 256
BLOCKS = 16
CAP = 48
STATE = 9 * BLOCKS
ROWS = STATE + 8
UNROLL = 4
VMEM_LIMIT = 48 * 1024 * 1024


def halves(x):
    high = x.astype(BF16)
    return high, (x - high.astype(F32)).astype(BF16)


def thirds(x):
    high = x.astype(BF16)
    rest = x - high.astype(F32)
    middle = rest.astype(BF16)
    return high, middle, (rest - middle.astype(F32)).astype(BF16)


def moment_of(b, l):
    return [
        b[0] * l[0],
        b[1] * l[1],
        b[2] * l[2],
        0.5 * (b[1] * l[2] + b[2] * l[1]),
        0.5 * (b[0] * l[2] + b[2] * l[0]),
        0.5 * (b[0] * l[1] + b[1] * l[0]),
    ]


def force_of(stress, b, l):
    xx, yy, zz, yz, xz, xy = stress
    px = xx * b[0] + xy * b[1] + xz * b[2]
    py = xy * b[0] + yy * b[1] + yz * b[2]
    pz = xz * b[0] + yz * b[1] + zz * b[2]
    return [py * l[2] - pz * l[1], pz * l[0] - px * l[2], px * l[1] - py * l[0]]


def iota(shape, dim):
    return lax.broadcasted_iota(I32, shape, dim)


def steps_of(slot):
    first = (slot >= 9).astype(I32) + (slot >= 18).astype(I32)
    rest = slot - 9 * first
    second = (rest >= 3).astype(I32) + (rest >= 6).astype(I32)
    return first, second, rest - 3 * second


def message_kernel(count, tree, offsets, burgers, segvec, cells, pairs, out):
    for block in range(BLOCKS):
        at = slice(block * WIDTH, (block + 1) * WIDTH)
        for part, ref in enumerate((offsets, burgers, segvec)):
            for member in range(3):
                row = (3 * part + member) * BLOCKS + block
                out[row : row + 1, :] = ref[member : member + 1, at]
    b = [out[(3 + m) * BLOCKS : (4 + m) * BLOCKS, :] for m in range(3)]
    l = [out[(6 + m) * BLOCKS : (7 + m) * BLOCKS, :] for m in range(3)]
    sums = [jnp.sum(m, axis=1, keepdims=True) for m in moment_of(b, l)]
    lane, sub = iota((BLOCKS, 128), 1), iota((BLOCKS, 128), 0)
    cell_row = jnp.concatenate([cells[...], jnp.zeros((1, 128 - BLOCKS), I32)], axis=1)
    cell = jnp.sum(jnp.where(lane == sub, cell_row.astype(F32), 0.0), axis=1, keepdims=True)
    chosen = jnp.zeros((BLOCKS, 128), F32)
    for member, total in enumerate(sums):
        chosen = jnp.where(lane // 8 == member, total, chosen)
    chosen = jnp.where(cell == (lane % 8).astype(F32), chosen, 0.0)
    source = jnp.sum(chosen, axis=0, keepdims=True)
    row_lane = iota((1, 128), 1)
    source = jnp.where(row_lane == 48, tree[0].astype(F32), source)

    listing = jnp.concatenate([pairs[...], jnp.zeros((3, 128 - CAP), I32)], axis=1)
    step_x, step_y, step_z = steps_of(listing[1:2])
    key = (
        jnp.where(step_z == 0, 4, 0) + jnp.where(step_y == 0, 2, 0) + jnp.where(step_x == 0, 1, 0)
    )
    key = jnp.where(row_lane < count[0], key, 8).astype(F32)
    wide_lane, wide_sub = iota((128, 128), 1), iota((128, 128), 0)
    key_down = jnp.sum(jnp.where(wide_lane == wide_sub, key, 0.0), axis=1, keepdims=True)
    starts = jnp.sum((key_down < wide_lane.astype(F32)).astype(F32), axis=0, keepdims=True)
    ahead = (key < key_down) | ((key == key_down) & (wide_lane < wide_sub))
    rank_down = jnp.sum(ahead.astype(F32), axis=1, keepdims=True)
    place = (rank_down == wide_lane.astype(F32)).astype(BF16)
    padded = jnp.concatenate([listing.astype(F32), jnp.zeros((5, 128), F32)], axis=0)
    order = jnp.dot(padded.astype(BF16), place, preferred_element_type=F32)
    rows = jnp.concatenate(
        [order[:3], starts, cell_row.astype(F32), source, jnp.zeros((2, 128), F32)], axis=0
    )
    out[STATE:, :] = jnp.concatenate([rows, jnp.zeros((8, 128), F32)], axis=1)


def column(values):
    row = iota((8, 1), 0)
    out = jnp.zeros((8, 1), F32)
    for index, value in enumerate(values):
        if value:
            out = jnp.where(row == index, value, out)
    return out


def features(moment, y):
    first = [moment * v for v in y]
    second = [
        first[0] * y[0],
        first[1] * y[1],
        first[2] * y[2],
        first[1] * y[2],
        first[0] * y[2],
        first[0] * y[1],
    ]
    return halves(jnp.concatenate([moment] + first + second, axis=0))


def contract(sums, x):
    s0, s1, s2, s3, xx, yy, zz, yz, xz, xy = [sums[8 * i : 8 * i + 8] for i in range(10)]
    ux, uy, uz = s1 - x[0] * s0, s2 - x[1] * s0, s3 - x[2] * s0
    xx = xx - x[0] * (s1 + ux)
    yy = yy - x[1] * (s2 + uy)
    zz = zz - x[2] * (s3 + uz)
    yz = yz - x[1] * s3 - x[2] * uy
    xz = xz - x[0] * s3 - x[2] * ux
    xy = xy - x[0] * s2 - x[1] * ux
    row = iota((8, 1), 0)

    def pick(*terms):
        out = 0.0
        for group, at in terms:
            out = jnp.where(row == at, group, out)
        return out

    def move(value, by):
        return pltpu.roll(value, by % 8, 0)

    out = (
        CORE * s0
        + xx * column([-2, 1, 1, 1, -0.5, -0.5])
        + yy * column([1, -2, 1, -0.5, 1, -0.5])
        + zz * column([1, 1, -2, -0.5, -0.5, 1])
    )
    edge = pick((yz, 3), (xz, 4), (xy, 5))
    out += -3.0 * (
        move(jnp.where((row == 4) | (row == 5), edge, 0.0), -4)
        + move(jnp.where(row == 5, edge, 0.0), -5)
        + move(jnp.where((row == 3) | (row == 4), edge, 0.0), -2)
        + move(jnp.where(row == 3, edge, 0.0), -1)
    )
    out += -1.5 * (
        move(pick((xz, 5)), -2)
        + move(pick((xy, 4), (yz, 5)), -1)
        + move(pick((yz, 2), (xy, 3), (yz, 4)), 1)
        + move(pick((yz, 1), (xz, 2), (xz, 3)), 2)
        + move(pick((xz, 0), (xy, 1)), 4)
        + move(pick((xy, 0)), 5)
    )
    return out


def block_pair(moment_i, x, moment_j, y, apart):
    row = iota((8, 1), 0)
    xs = [x[c] + apart[c] for c in range(3)]
    ys = [y[c] - apart[c] for c in range(3)]
    norm_x = xs[0] * xs[0] + xs[1] * xs[1] + xs[2] * xs[2] + CORE
    norm_y = y[0] * y[0] + y[1] * y[1] + y[2] * y[2]
    left, right = jnp.where(row == 4, 1.0, 0.0), jnp.where(row == 3, 1.0, 0.0)
    for index, (a, b) in enumerate(zip(xs + [norm_x], y)):
        left = jnp.where(row == index, -2.0 * a, left)
        right = jnp.where(row == index, b, right)
    left = jnp.where(row == 3, norm_x, left)
    right = jnp.where(row == 4, norm_y, right)
    l1, l2, l3 = thirds(left)
    r1, r2, r3 = thirds(right)
    square = lax.dot_general(
        jnp.concatenate([l1, l1, l2, l2, l1, l3], axis=0),
        jnp.concatenate([r1, r2, r1, r2, r3, r1], axis=0),
        (((0,), (0,)), ((), ())),
        preferred_element_type=F32,
    )
    inverse = lax.rsqrt(square)
    second = inverse * inverse
    high, low = halves(second * second * inverse)

    def apply(moment, at, dims):
        f_high, f_low = features(moment, at)
        count = f_high.shape[0]
        both = lax.dot_general(
            jnp.concatenate([f_high, f_low], axis=0), high, dims, preferred_element_type=F32
        )
        rest = lax.dot_general(f_high, low, dims, preferred_element_type=F32)
        return both[:count] + both[count:] + rest

    on_i = contract(apply(moment_j, y, (((1,), (1,)), ((), ()))), xs)
    on_j = contract(apply(moment_i, x, (((1,), (0,)), ((), ()))), ys)
    return on_i, on_j


def near_kernel(ints, near, beyond, out_near, out_beyond, moments, stress, todo):
    def rows_of(ref, at):
        return jnp.concatenate([ref[0, at, :], ref[1, at, :]], axis=1)

    def fill(domain, carry):
        for half, ref in enumerate((near, beyond)):
            b = [ref[domain, (3 + m) * BLOCKS : (4 + m) * BLOCKS, :] for m in range(3)]
            l = [ref[domain, (6 + m) * BLOCKS : (7 + m) * BLOCKS, :] for m in range(3)]
            base = (half * 4 + domain) * BLOCKS * 8
            zero = jnp.zeros((BLOCKS, WIDTH), F32)
            for member, value in enumerate(moment_of(b, l) + [zero, zero]):
                at = pl.ds(base + member, BLOCKS, stride=8)
                moments[0, at, :] = value[:, :128]
                moments[1, at, :] = value[:, 128:]
        return carry

    lax.fori_loop(0, 4, fill, 0)
    stress[...] = jnp.zeros_like(stress)

    total = jnp.int32(0)
    for domain in range(8):
        start, end = ints[domain * 8 + 3, domain], ints[domain * 8 + 3, domain + 1]

        def put(k, carry, domain=domain, start=start, total=total):
            todo[total + k - start] = domain * 64 + k
            return carry

        lax.fori_loop(start, end, put, 0)
        total = total + (end - start)

    def offsets_of(domain, block):
        out = []
        for member in range(3):
            at = pl.ds(member * BLOCKS + block, 1)
            value = jnp.where(
                domain >= 4, beyond[domain & 3, at, :], near[domain & 3, at, :]
            )
            out.append(jnp.broadcast_to(value, (8, WIDTH)))
        return out

    def one(index):
        live = index < total
        item = todo[jnp.where(live, index, 0)]
        domain, k = item >> 6, item & 63
        first = ints[domain * 8, k]
        slot = ints[domain * 8 + 1, k]
        second = ints[domain * 8 + 2, k]
        step_x = (slot * 57) >> 9
        rest = slot - 9 * step_x
        step_y = (rest * 11) >> 5
        step_z = rest - 3 * step_y
        steps = [step_x - 1, step_y - 1, step_z - 1]
        other = domain + steps[0] + 2 * steps[1] + 4 * steps[2]
        cell_i, cell_j = ints[domain * 8 + 4, first], ints[other * 8 + 4, second]
        apart = []
        for member in range(3):
            bit = 2 - member
            gap = ((cell_i >> bit) & 1) - ((cell_j >> bit) & 1) - 2 * steps[member]
            apart.append(0.5 * gap.astype(F32))
        at_i, at_j = domain * BLOCKS + first, other * BLOCKS + second
        on_i, on_j = block_pair(
            rows_of(moments, pl.ds(pl.multiple_of(at_i * 8, 8), 8)),
            offsets_of(domain, first),
            rows_of(moments, pl.ds(pl.multiple_of(at_j * 8, 8), 8)),
            offsets_of(other, second),
            apart,
        )
        spare = 8 * BLOCKS
        return jnp.where(live, at_i, spare), jnp.where(live, at_j, spare), on_i, on_j

    def several(turn, carry):
        results = [one(turn * UNROLL + index) for index in range(UNROLL)]
        for at_i, at_j, on_i, on_j in results:
            for at, value in ((at_i, on_i), (at_j, on_j)):
                at = pl.ds(pl.multiple_of(at * 8, 8), 8)
                stress[0, at, :] += value[:, :128]
                stress[1, at, :] += value[:, 128:]
        return carry

    lax.fori_loop(0, (total + (UNROLL - 1)) // UNROLL, several, 0)

    def finish(domain, carry):
        for half, (ref, out) in enumerate(((near, out_near), (beyond, out_beyond))):
            b = [ref[domain, (3 + m) * BLOCKS : (4 + m) * BLOCKS, :] for m in range(3)]
            l = [ref[domain, (6 + m) * BLOCKS : (7 + m) * BLOCKS, :] for m in range(3)]
            base = (half * 4 + domain) * BLOCKS * 8
            total = [rows_of(stress, pl.ds(base + m, BLOCKS, stride=8)) for m in range(6)]
            for member, value in enumerate(force_of(total, b, l)):
                out[domain, member * BLOCKS : (member + 1) * BLOCKS, :] = value
        return carry

    lax.fori_loop(0, 4, finish, 0)


def final_kernel(message, near, sources, out):
    lane = iota((128, 128), 1)
    expand_row, expand_lane = iota((128, 7 * 128), 0), iota((128, 7 * 128), 1)
    member = expand_lane // 128
    inner = expand_lane % 128
    wanted = jnp.where(member == 6, 48, member * 8 + inner % 8)
    expand = (expand_row == wanted).astype(BF16)
    spread = sum(
        jnp.dot(part, expand, preferred_element_type=F32) for part in thirds(sources[...])
    )
    values = [spread[:, 128 * m : 128 * (m + 1)] for m in range(7)]
    tree = values[6]
    index = iota((128, 128), 0)
    rel_x = (index & 1) + 2 * ((index >> 3) & 1)
    rel_y = ((index >> 1) & 1) + 2 * ((index >> 4) & 1)
    rel_z = ((index >> 2) & 1) + 2 * ((index >> 5) & 3)
    steps = [
        jnp.where(rel_x > 2, rel_x - 4, rel_x),
        jnp.where(rel_y > 2, rel_y - 4, rel_y),
        jnp.where(rel_z > 4, rel_z - 8, rel_z),
    ]
    apart = functools.reduce(jnp.maximum, [jnp.abs(s) for s in steps])
    mask = ((apart > 1) & (lane < 64)).astype(F32)
    target, source = lane >> 3, lane & 7
    r = []
    for m in range(3):
        bit = 2 - m
        at = 0.25 + 0.5 * ((target >> bit) & 1).astype(F32)
        own = 0.25 + 0.5 * ((source >> bit) & 1).astype(F32)
        r.append(at - (jnp.where(tree == 1.0, own, 0.5) + steps[m].astype(F32)))
    xx, yy, zz, yz, xz, xy = [values[m] * mask for m in range(6)]
    inverse = lax.rsqrt(r[0] * r[0] + r[1] * r[1] + r[2] * r[2] + CORE)
    cubed = inverse * inverse * inverse
    weight = 3.0 * cubed * inverse * inverse
    ax = xx * r[0] + xy * r[1] + xz * r[2]
    ay = xy * r[0] + yy * r[1] + yz * r[2]
    az = xz * r[0] + yz * r[1] + zz * r[2]
    stress = [
        xx * cubed - weight * ax * r[0],
        yy * cubed - weight * ay * r[1],
        zz * cubed - weight * az * r[2],
        yz * cubed - 0.5 * weight * (ay * r[2] + az * r[1]),
        xz * cubed - 0.5 * weight * (ax * r[2] + az * r[0]),
        xy * cubed - 0.5 * weight * (ax * r[1] + ay * r[0]),
    ]
    block_lane, block_sub = iota((BLOCKS, 128), 1), iota((BLOCKS, 128), 0)
    cells = message[STATE + 4 : STATE + 5, 0:128]
    cell = jnp.sum(jnp.where(block_lane == block_sub, cells, 0.0), axis=1, keepdims=True)
    mine = (block_lane >> 3).astype(F32) == cell
    by_block = []
    for value in stress:
        row = jnp.sum(value, axis=0, keepdims=True)
        by_block.append(jnp.sum(jnp.where(mine, row, 0.0), axis=1, keepdims=True))
    b = [message[(3 + m) * BLOCKS : (4 + m) * BLOCKS, :] for m in range(3)]
    l = [message[(6 + m) * BLOCKS : (7 + m) * BLOCKS, :] for m in range(3)]
    for m, value in enumerate(force_of(by_block, b, l)):
        value = value + near[m * BLOCKS : (m + 1) * BLOCKS, :]
        for block in range(BLOCKS):
            out[m : m + 1, block * WIDTH : (block + 1) * WIDTH] = value[block : block + 1]


def in_vmem(count):
    return [pl.BlockSpec(memory_space=pltpu.VMEM)] * count


def in_smem(count):
    return [pl.BlockSpec(memory_space=pltpu.SMEM)] * count


PARAMS = pltpu.CompilerParams(vmem_limit_bytes=VMEM_LIMIT)


def make_message(count, tree, offsets, burgers, segvec, cells, pairs):
    return pl.pallas_call(
        message_kernel,
        out_shape=jax.ShapeDtypeStruct((ROWS, WIDTH), F32),
        in_specs=in_smem(2) + in_vmem(5),
        out_specs=in_vmem(1)[0],
        compiler_params=PARAMS,
    )(count, tree, offsets, burgers, segvec, cells, pairs)


def near_forces(ints, near, beyond):
    shape = jax.ShapeDtypeStruct((4, 3 * BLOCKS, WIDTH), F32)
    return pl.pallas_call(
        near_kernel,
        out_shape=(shape, shape),
        in_specs=in_smem(1) + in_vmem(2),
        out_specs=tuple(in_vmem(2)),
        scratch_shapes=[
            pltpu.VMEM((2, 8 * BLOCKS * 8, 128), F32),
            pltpu.VMEM((2, (8 * BLOCKS + 1) * 8, 128), F32),
            pltpu.SMEM((8 * CAP + 8,), I32),
        ],
        compiler_params=PARAMS,
    )(ints, near, beyond)


def final_forces(message, near, sources, length):
    return pl.pallas_call(
        final_kernel,
        out_shape=jax.ShapeDtypeStruct((3, length), F32),
        in_specs=in_vmem(3),
        out_specs=in_vmem(1)[0],
        compiler_params=PARAMS,
    )(message, near, sources)


def from_ahead(x, axis, by):
    size = lax.axis_size(axis)
    return lax.ppermute(x, axis, [(i, (i - by) % size) for i in range(size)])


def to_ahead(x, axis):
    size = lax.axis_size(axis)
    return lax.ppermute(x, axis, [(i, (i + 1) % size) for i in range(size)])


def shards(offsets, burgers, segvec, block_cell, tree_level, pair_count, pair_list):
    message = make_message(
        pair_count,
        tree_level,
        offsets[0, 0, 0],
        burgers[0, 0, 0],
        segvec[0, 0, 0],
        block_cell[0, 0],
        pair_list[0, 0, 0],
    )
    line = jnp.stack([message, from_ahead(message, "gx", 1)])
    near = jnp.concatenate([line, from_ahead(line, "gy", 1)])
    beyond = from_ahead(near, "gz", 1)
    ints = jnp.concatenate([near[:, STATE:, :128], beyond[:, STATE:, :128]])
    sources = ints[:, 5]
    ints = ints.astype(I32).reshape(64, 128)
    for axis, by in (("gx", 2), ("gy", 2), ("gz", 2), ("gz", 4)):
        sources = jnp.concatenate([sources, from_ahead(sources, axis, by)])
    force_near, force_beyond = near_forces(ints, near, beyond)
    force = force_near + to_ahead(force_beyond, "gz")
    force = force[:2] + to_ahead(force[2:], "gy")
    force = force[0] + to_ahead(force[1], "gx")
    total = final_forces(message, force, sources, offsets.shape[-1])
    return total[None, None, None]


def solution(mesh):
    in_specs = (
        P("gx", "gy", "gz", None, None),
        P("gx", "gy", "gz", None, None),
        P("gx", "gy", "gz", None, None),
        P("gx", "gy", "gz", None),
        P(("gx", "gy", "gz")),
        P(("gx", "gy", "gz")),
        P("gx", "gy", "gz", None, None),
    )
    out_specs = P("gx", "gy", "gz", None, None)
    return jax.shard_map(shards, mesh=mesh, in_specs=in_specs, out_specs=out_specs, check_vma=False)
```

```python
import functools

import jax
import jax.numpy as jnp
from jax import lax
from jax.experimental import pallas as pl
from jax.experimental.pallas import tpu as pltpu
from jax.sharding import PartitionSpec as P

F32, BF16, I32 = jnp.float32, jnp.bfloat16, jnp.int32
CORE = 0.04
LANES = 128
WIDTH = 256
BLOCKS = 16
CAP = 48
PART = 3 * 2 * BLOCKS
STATE = 3 * PART
ROWS = STATE + 8
KINDS = 12
MANY, FEW = 8, 4
VMEM_LIMIT = 48 * 1024 * 1024


def halves(x):
    high = x.astype(BF16)
    return high, (x - high.astype(F32)).astype(BF16)


def thirds(x):
    high = x.astype(BF16)
    rest = x - high.astype(F32)
    middle = rest.astype(BF16)
    return high, middle, (rest - middle.astype(F32)).astype(BF16)


def moment_of(b, l):
    return [
        b[0] * l[0],
        b[1] * l[1],
        b[2] * l[2],
        0.5 * (b[1] * l[2] + b[2] * l[1]),
        0.5 * (b[0] * l[2] + b[2] * l[0]),
        0.5 * (b[0] * l[1] + b[1] * l[0]),
    ]


def force_of(stress, b, l):
    xx, yy, zz, yz, xz, xy = stress
    px = xx * b[0] + xy * b[1] + xz * b[2]
    py = xy * b[0] + yy * b[1] + yz * b[2]
    pz = xz * b[0] + yz * b[1] + zz * b[2]
    return [py * l[2] - pz * l[1], pz * l[0] - px * l[2], px * l[1] - py * l[0]]


def iota(shape, dim):
    return lax.broadcasted_iota(I32, shape, dim)


def steps_of(slot):
    first = (slot >= 9).astype(I32) + (slot >= 18).astype(I32)
    rest = slot - 9 * first
    second = (rest >= 3).astype(I32) + (rest >= 6).astype(I32)
    return first, second, rest - 3 * second


def half_rows(ref, base, half):
    return [ref[pl.ds(base + m * 2 * BLOCKS + half, BLOCKS, stride=2), :] for m in range(3)]


def message_kernel(raw, out, far):
    notes = raw[STATE:, :]
    sums = [jnp.zeros((BLOCKS, 1), F32)] * 6
    for half in range(2):
        moments = moment_of(half_rows(raw, PART, half), half_rows(raw, 2 * PART, half))
        sums = [a + jnp.sum(m, axis=1, keepdims=True) for a, m in zip(sums, moments)]
    lane, sub = iota((BLOCKS, LANES), 1), iota((BLOCKS, LANES), 0)
    cell_row = notes[3:4]
    cell = jnp.sum(jnp.where(lane == sub, cell_row, 0.0), axis=1, keepdims=True)
    chosen = cell == lane.astype(F32)
    rows = [jnp.sum(jnp.where(chosen, v, 0.0), axis=0, keepdims=True) for v in sums]
    rows.append(notes[5:6])
    rows.append(jnp.zeros((1, LANES), F32))
    far[...] = jnp.concatenate(rows, axis=0)

    step_x, step_y, step_z = steps_of(notes[1:2].astype(I32))
    key = jnp.where(step_y == 0, 2, 0) + jnp.where(step_x == 0, 1, 0)
    key = key + jnp.where(step_z == 0, 8, jnp.where(step_z == 2, 4, 0))
    row_lane = iota((1, LANES), 1)
    key = jnp.where(row_lane.astype(F32) < notes[4:5], key, KINDS).astype(F32)
    wide_lane, wide_sub = iota((LANES, LANES), 1), iota((LANES, LANES), 0)
    key_down = jnp.sum(jnp.where(wide_lane == wide_sub, key, 0.0), axis=1, keepdims=True)
    starts = jnp.sum((key_down < wide_lane.astype(F32)).astype(F32), axis=0, keepdims=True)
    ahead = (key < key_down) | ((key == key_down) & (wide_lane < wide_sub))
    rank_down = jnp.sum(ahead.astype(F32), axis=1, keepdims=True)
    place = (rank_down == wide_lane.astype(F32)).astype(BF16)
    order = jnp.dot(notes.astype(BF16), place, preferred_element_type=F32)
    out[...] = jnp.concatenate(
        [order[:3], starts, cell_row, jnp.zeros((3, LANES), F32)], axis=0
    )


def column(values):
    row = iota((8, 1), 0)
    out = jnp.zeros((8, 1), F32)
    for index, value in enumerate(values):
        if value:
            out = jnp.where(row == index, value, out)
    return out


def features(moment, y):
    first = [moment * v for v in y]
    second = [
        first[0] * y[0],
        first[1] * y[1],
        first[2] * y[2],
        first[1] * y[2],
        first[0] * y[2],
        first[0] * y[1],
    ]
    return halves(jnp.concatenate([moment] + first + second, axis=0))


def contract(sums, x):
    s0, s1, s2, s3, xx, yy, zz, yz, xz, xy = [sums[8 * i : 8 * i + 8] for i in range(10)]
    ux, uy, uz = s1 - x[0] * s0, s2 - x[1] * s0, s3 - x[2] * s0
    xx = xx - x[0] * (s1 + ux)
    yy = yy - x[1] * (s2 + uy)
    zz = zz - x[2] * (s3 + uz)
    yz = yz - x[1] * s3 - x[2] * uy
    xz = xz - x[0] * s3 - x[2] * ux
    xy = xy - x[0] * s2 - x[1] * ux
    row = iota((8, 1), 0)

    def pick(*terms):
        out = 0.0
        for group, at in terms:
            out = jnp.where(row == at, group, out)
        return out

    def move(value, by):
        return pltpu.roll(value, by % 8, 0)

    out = (
        CORE * s0
        + xx * column([-2, 1, 1, 1, -0.5, -0.5])
        + yy * column([1, -2, 1, -0.5, 1, -0.5])
        + zz * column([1, 1, -2, -0.5, -0.5, 1])
    )
    edge = pick((yz, 3), (xz, 4), (xy, 5))
    out += -3.0 * (
        move(jnp.where((row == 4) | (row == 5), edge, 0.0), -4)
        + move(jnp.where(row == 5, edge, 0.0), -5)
        + move(jnp.where((row == 3) | (row == 4), edge, 0.0), -2)
        + move(jnp.where(row == 3, edge, 0.0), -1)
    )
    out += -1.5 * (
        move(pick((xz, 5)), -2)
        + move(pick((xy, 4), (yz, 5)), -1)
        + move(pick((yz, 2), (xy, 3), (yz, 4)), 1)
        + move(pick((yz, 1), (xz, 2), (xz, 3)), 2)
        + move(pick((xz, 0), (xy, 1)), 4)
        + move(pick((xy, 0)), 5)
    )
    return out


NT = (((1,), (1,)), ((), ()))
NN = (((1,), (0,)), ((), ()))


def weights(x, y, apart):
    row = iota((8, 1), 0)
    xs = [x[c] + apart[c] for c in range(3)]
    norm_x = xs[0] * xs[0] + xs[1] * xs[1] + xs[2] * xs[2] + CORE
    norm_y = y[0] * y[0] + y[1] * y[1] + y[2] * y[2]
    left, right = jnp.where(row == 4, 1.0, 0.0), jnp.where(row == 3, 1.0, 0.0)
    for index in range(3):
        left = jnp.where(row == index, -2.0 * xs[index], left)
        right = jnp.where(row == index, y[index], right)
    left = jnp.where(row == 3, norm_x, left)
    right = jnp.where(row == 4, norm_y, right)
    l1, l2, l3 = thirds(left)
    r1, r2, r3 = thirds(right)
    square = lax.dot_general(
        jnp.concatenate([l1, l1, l2, l2, l1, l3], axis=0),
        jnp.concatenate([r1, r2, r1, r2, r3, r1], axis=0),
        (((0,), (0,)), ((), ())),
        preferred_element_type=F32,
    )
    inverse = lax.rsqrt(square)
    second = inverse * inverse
    return halves(second * second * inverse)


def apply(moment, at, high, low, dims):
    f_high, f_low = features(moment, at)
    count = f_high.shape[0]
    both = lax.dot_general(
        jnp.concatenate([f_high, f_low], axis=0), high, dims, preferred_element_type=F32
    )
    rest = lax.dot_general(f_high, low, dims, preferred_element_type=F32)
    return both[:count] + both[count:] + rest


def rows_of(ref, at):
    return jnp.concatenate([ref[0, at, :], ref[1, at, :]], axis=1)


def tile(block):
    return pl.ds(pl.multiple_of(block * 8, 8), 8)


def fill_moments(ref, moments):
    def fill(domain, carry):
        for half in range(2):
            b = half_rows(ref, domain * ROWS + PART, half)
            l = half_rows(ref, domain * ROWS + 2 * PART, half)
            zero = jnp.zeros((BLOCKS, LANES), F32)
            for member, value in enumerate(moment_of(b, l) + [zero, zero]):
                at = pl.ds(domain * BLOCKS * 8 + member, BLOCKS, stride=8)
                moments[half, at, :] = value
        return carry

    lax.fori_loop(0, 4, fill, 0)


def finish(ref, stress, far, out):
    def one(domain, carry):
        base = domain * ROWS
        if far is not None:
            lane, sub = iota((BLOCKS, LANES), 1), iota((BLOCKS, LANES), 0)
            cells = ref[pl.ds(base + STATE + 4, 1), :]
            cell = jnp.sum(jnp.where(lane == sub, cells, 0.0), axis=1, keepdims=True)
            chosen = cell + (far[1] + domain * 8).astype(F32) == lane.astype(F32)
            extra = [
                jnp.sum(jnp.where(chosen, v, 0.0), axis=1, keepdims=True) for v in far[0]
            ]
        for half in range(2):
            b = half_rows(ref, base + PART, half)
            l = half_rows(ref, base + 2 * PART, half)
            rows = [pl.ds(domain * BLOCKS * 8 + m, BLOCKS, stride=8) for m in range(6)]
            total = [stress[half, at, :] for at in rows]
            if far is not None:
                total = [v + e for v, e in zip(total, extra)]
            for member, value in enumerate(force_of(total, b, l)):
                at = pl.ds(domain * PART + member * 2 * BLOCKS + half, BLOCKS, stride=2)
                out[at, :] = value
        return carry

    lax.fori_loop(0, 4, one, 0)


def offsets_of(ref, domain, block):
    out = []
    for member in range(3):
        at = domain * ROWS + member * 2 * BLOCKS + 2 * block
        out.append(
            jnp.concatenate(
                [jnp.broadcast_to(ref[pl.ds(at + h, 1), :], (8, LANES)) for h in range(2)], axis=1
            )
        )
    return out


def all_pairs(ints, groups, todo, left, right, left_stress, right_stress, high, low):
    total = jnp.int32(0)
    for kind, domain in groups:
        start, end = ints[domain * 8 + 3, kind], ints[domain * 8 + 3, kind + 1]

        def put(k, carry, domain=domain, start=start, total=total):
            todo[total + k - start] = domain * 64 + k
            return carry

        lax.fori_loop(start, end, put, 0)
        total = total + (end - start)
    crossing = any(domain >= 4 for _, domain in groups)

    def find(index):
        live = index < total
        item = todo[jnp.where(live, index, 0)]
        domain, k = item >> 6, item & 63
        first = ints[domain * 8, k]
        slot = ints[domain * 8 + 1, k]
        second = ints[domain * 8 + 2, k]
        step_x = (slot * 57) >> 9
        rest = slot - 9 * step_x
        step_y = (rest * 11) >> 5
        step_z = rest - 3 * step_y
        steps = [step_x - 1, step_y - 1, step_z - 1]
        other = domain + steps[0] + 2 * steps[1] + 4 * steps[2]
        cell_i, cell_j = ints[domain * 8 + 4, first], ints[other * 8 + 4, second]
        sign = jnp.where(domain < 4, 0.5, -0.5) if crossing else 0.5
        apart = []
        for member in range(3):
            bit = 2 - member
            gap = ((cell_i >> bit) & 1) - ((cell_j >> bit) & 1) - 2 * steps[member]
            apart.append(sign * gap.astype(F32))
        i, j = (domain, first), (other, second)
        if crossing:
            swap = domain >= 4
            i, j = (
                [jnp.where(swap, b, a) for a, b in zip(i, j)],
                [jnp.where(swap, a, b) for a, b in zip(i, j)],
            )
            j = (j[0] - 4, j[1])
        spare = 4 * BLOCKS
        at_i, at_j = i[0] * BLOCKS + i[1], j[0] * BLOCKS + j[1]
        return i, j, at_i, at_j, jnp.where(live, at_i, spare), jnp.where(live, at_j, spare), apart

    def work(base, count):
        found = [find(base + index) for index in range(count)]
        for index, (i, j, _, _, _, _, apart) in enumerate(found):
            parts = weights(offsets_of(left[0], *i), offsets_of(right[0], *j), apart)
            high[index], low[index] = parts
        for index, (i, j, at_i, at_j, to_i, to_j, apart) in enumerate(found):
            x, y = offsets_of(left[0], *i), offsets_of(right[0], *j)
            xs = [x[c] + apart[c] for c in range(3)]
            ys = [y[c] - apart[c] for c in range(3)]
            moment_i, moment_j = rows_of(left[1], tile(at_i)), rows_of(right[1], tile(at_j))
            on_i = contract(apply(moment_j, y, high[index], low[index], NT), xs)
            on_j = contract(apply(moment_i, x, high[index], low[index], NN), ys)
            for ref, to, value in ((left_stress, to_i, on_i), (right_stress, to_j, on_j)):
                ref[0, tile(to), :] += value[:, :LANES]
                ref[1, tile(to), :] += value[:, LANES:]

    whole, rest = total >> 3, total & 7
    rounds = whole + (rest > FEW).astype(I32)

    def many(turn, carry):
        work(turn * MANY, MANY)
        return carry

    def few(turn, carry):
        work(whole * MANY, FEW)
        return carry

    lax.fori_loop(0, rounds, many, 0)
    lax.fori_loop(0, ((rest > 0) & (rest <= FEW)).astype(I32), few, 0)


def inner_kernel(ints, near, out, moments, stress, high, low, todo):
    fill_moments(near, moments)
    stress[...] = jnp.zeros_like(stress)
    both = (near, moments)
    groups = [(d, d) for d in range(4)]
    all_pairs(ints, groups, todo, both, both, stress, stress, high, low)
    finish(near, stress, None, out)


def crossing_kernel(ints, near, beyond, near_stress, beyond_stress, near_moments, beyond_moments, high, low, todo):
    fill_moments(near, near_moments)
    fill_moments(beyond, beyond_moments)
    near_stress[...] = jnp.zeros_like(near_stress)
    beyond_stress[...] = jnp.zeros_like(beyond_stress)
    groups = [(4 + d, d) for d in range(4)] + [(8 + d, 4 + d) for d in range(4)]
    left, right = (near, near_moments), (beyond, beyond_moments)
    all_pairs(ints, groups, todo, left, right, near_stress, beyond_stress, high, low)


def force_kernel(near, beyond, near_stress, beyond_stress, sources, out_near, out_beyond):
    far = far_field(sources[...])
    finish(beyond, beyond_stress, (far, 32), out_beyond)
    finish(near, near_stress, (far, 0), out_near)


def far_field(sources):
    row, lane = iota((64, LANES), 0), iota((64, LANES), 1)
    steps = []
    for member, size in enumerate((4, 4, 8)):
        place = 2 * ((lane >> (5, 6, 3)[member]) & 1)
        if member == 2:
            place = place + 4 * ((lane >> 4) & 1)
        step = place - ((row >> (3 + member)) & 1)
        steps.append(jnp.where(step > size // 2, step - size, step))
    most = functools.reduce(jnp.maximum, [jnp.abs(s) for s in steps])
    mask = (most > 1).astype(F32)
    tree = sources[6:7]
    r = []
    for member in range(3):
        bit = 2 - member
        at = 0.25 + 0.5 * ((row >> bit) & 1).astype(F32)
        own = 0.25 + 0.5 * ((lane >> bit) & 1).astype(F32)
        r.append(at - (jnp.where(tree == 1.0, own, 0.5) + steps[member].astype(F32)))
    xx, yy, zz, yz, xz, xy = [sources[m : m + 1] * mask for m in range(6)]
    inverse = lax.rsqrt(r[0] * r[0] + r[1] * r[1] + r[2] * r[2] + CORE)
    cubed = inverse * inverse * inverse
    weight = 3.0 * cubed * inverse * inverse
    ax = xx * r[0] + xy * r[1] + xz * r[2]
    ay = xy * r[0] + yy * r[1] + yz * r[2]
    az = xz * r[0] + yz * r[1] + zz * r[2]
    stress = [
        xx * cubed - weight * ax * r[0],
        yy * cubed - weight * ay * r[1],
        zz * cubed - weight * az * r[2],
        yz * cubed - 0.5 * weight * (ay * r[2] + az * r[1]),
        xz * cubed - 0.5 * weight * (ax * r[2] + az * r[0]),
        xy * cubed - 0.5 * weight * (ax * r[1] + ay * r[0]),
    ]
    out = []
    for value in stress:
        total = jnp.sum(value, axis=1, keepdims=True)
        out.append(jnp.sum(jnp.where(row == lane, total, 0.0), axis=0, keepdims=True))
    return out


def in_vmem(count):
    return [pl.BlockSpec(memory_space=pltpu.VMEM)] * count


def in_smem(count):
    return [pl.BlockSpec(memory_space=pltpu.SMEM)] * count


PARAMS = pltpu.CompilerParams(vmem_limit_bytes=VMEM_LIMIT)


def make_message(raw):
    last = STATE // 8
    return pl.pallas_call(
        message_kernel,
        grid=(1,),
        out_shape=(
            jax.ShapeDtypeStruct((ROWS, LANES), F32),
            jax.ShapeDtypeStruct((8, LANES), F32),
        ),
        in_specs=[pl.BlockSpec((ROWS, LANES), lambda i: (0, 0))],
        out_specs=(
            pl.BlockSpec((8, LANES), lambda i: (last, 0)),
            pl.BlockSpec((8, LANES), lambda i: (0, 0)),
        ),
        input_output_aliases={0: 0},
        compiler_params=PARAMS,
    )(raw)


FORCES = jax.ShapeDtypeStruct((4 * PART, LANES), F32)


MOMENTS = pltpu.VMEM((2, 4 * BLOCKS * 8, LANES), F32)
STRESS = (2, (4 * BLOCKS + 1) * 8, LANES)
WORK = [pltpu.VMEM((MANY, WIDTH, WIDTH), BF16)] * 2 + [pltpu.SMEM((8 * CAP + 8,), I32)]


def inner_forces(ints, near):
    return pl.pallas_call(
        inner_kernel,
        out_shape=FORCES,
        in_specs=in_smem(1) + in_vmem(1),
        out_specs=in_vmem(1)[0],
        scratch_shapes=[MOMENTS, pltpu.VMEM(STRESS, F32)] + WORK,
        compiler_params=PARAMS,
        cost_estimate=pl.CostEstimate(flops=10**9, bytes_accessed=10**6, transcendentals=10**6),
    )(ints, near)


def crossing_stress(ints, near, beyond):
    return pl.pallas_call(
        crossing_kernel,
        out_shape=(jax.ShapeDtypeStruct(STRESS, F32),) * 2,
        in_specs=in_smem(1) + in_vmem(2),
        out_specs=tuple(in_vmem(2)),
        scratch_shapes=[MOMENTS] * 2 + WORK,
        compiler_params=PARAMS,
        cost_estimate=pl.CostEstimate(flops=10**9, bytes_accessed=10**6, transcendentals=10**6),
    )(ints, near, beyond)


def outer_forces(near, beyond, near_stress, beyond_stress, sources):
    return pl.pallas_call(
        force_kernel,
        out_shape=(FORCES, FORCES),
        in_specs=in_vmem(5),
        out_specs=tuple(in_vmem(2)),
        compiler_params=PARAMS,
    )(near, beyond, near_stress, beyond_stress, sources)


def from_ahead(x, axis, by):
    size = lax.axis_size(axis)
    return lax.ppermute(x, axis, [(i, (i - by) % size) for i in range(size)])


def to_ahead(x, axis):
    size = lax.axis_size(axis)
    return lax.ppermute(x, axis, [(i, (i + 1) % size) for i in range(size)])


def numbers(states):
    return states.reshape(-1, ROWS, LANES)[:, STATE:].reshape(-1, LANES).astype(I32)


def shards(offsets, burgers, segvec, block_cell, tree_level, pair_count, pair_list):
    notes = [
        jnp.pad(pair_list.reshape(3, CAP), ((0, 0), (0, LANES - CAP))),
        jnp.pad(block_cell.reshape(1, BLOCKS), ((0, 0), (0, LANES - BLOCKS))),
        jnp.broadcast_to(pair_count[None], (1, LANES)),
        jnp.broadcast_to(tree_level[None], (3, LANES)),
    ]
    raw = jnp.concatenate(
        [v.reshape(PART, LANES) for v in (offsets, burgers, segvec)]
        + [jnp.concatenate(notes).astype(F32)]
    )
    message, source = make_message(raw)
    sources = source[:, :8]

    def grown(sources, axis, by):
        return jnp.concatenate([sources, from_ahead(sources, axis, by)], axis=1)

    ahead = from_ahead(message, "gx", 1)
    ahead, sources = lax.optimization_barrier((ahead, grown(sources, "gz", 2)))
    line = jnp.concatenate([message, ahead])
    ahead = from_ahead(line, "gy", 1)
    ahead, sources = lax.optimization_barrier((ahead, grown(sources, "gz", 4)))
    near = jnp.concatenate([line, ahead])
    beyond = from_ahead(near, "gz", 1)
    near_ints = numbers(near)
    force = inner_forces(near_ints, near)
    beyond, sources, force = lax.optimization_barrier((beyond, grown(sources, "gx", 2), force))
    ints = jnp.concatenate([near_ints, numbers(beyond)])
    near_stress, beyond_stress = crossing_stress(ints, near, beyond)
    sources = grown(sources, "gy", 2)
    force_near, force_beyond = outer_forces(near, beyond, near_stress, beyond_stress, sources)
    force = force + force_near + to_ahead(force_beyond, "gz")
    force = force[: 2 * PART] + to_ahead(force[2 * PART :], "gy")
    force = force[:PART] + to_ahead(force[PART:], "gx")
    return force.reshape(offsets.shape)


def solution(mesh):
    in_specs = (
        P("gx", "gy", "gz", None, None),
        P("gx", "gy", "gz", None, None),
        P("gx", "gy", "gz", None, None),
        P("gx", "gy", "gz", None),
        P(("gx", "gy", "gz")),
        P(("gx", "gy", "gz")),
        P("gx", "gy", "gz", None, None),
    )
    out_specs = P("gx", "gy", "gz", None, None)
    return jax.shard_map(shards, mesh=mesh, in_specs=in_specs, out_specs=out_specs, check_vma=False)
```

```python
import functools

import jax
import jax.numpy as jnp
from jax import lax
from jax.experimental import pallas as pl
from jax.experimental.pallas import tpu as pltpu
from jax.sharding import PartitionSpec as P

F32, BF16, I32 = jnp.float32, jnp.bfloat16, jnp.int32
CORE = 0.04
LANES = 128
WIDTH = 256
BLOCKS = 16
CAP = 48
PART = 3 * 2 * BLOCKS
STATE = 3 * PART
ROWS = STATE + 8
KINDS = 12
MANY, FEW = 8, 4
VMEM_LIMIT = 48 * 1024 * 1024


def halves(x):
    high = x.astype(BF16)
    return high, (x - high.astype(F32)).astype(BF16)


def thirds(x):
    high = x.astype(BF16)
    rest = x - high.astype(F32)
    middle = rest.astype(BF16)
    return high, middle, (rest - middle.astype(F32)).astype(BF16)


def moment_of(b, l):
    return [
        b[0] * l[0],
        b[1] * l[1],
        b[2] * l[2],
        0.5 * (b[1] * l[2] + b[2] * l[1]),
        0.5 * (b[0] * l[2] + b[2] * l[0]),
        0.5 * (b[0] * l[1] + b[1] * l[0]),
    ]


def force_of(stress, b, l):
    xx, yy, zz, yz, xz, xy = stress
    px = xx * b[0] + xy * b[1] + xz * b[2]
    py = xy * b[0] + yy * b[1] + yz * b[2]
    pz = xz * b[0] + yz * b[1] + zz * b[2]
    return [py * l[2] - pz * l[1], pz * l[0] - px * l[2], px * l[1] - py * l[0]]


def iota(shape, dim):
    return lax.broadcasted_iota(I32, shape, dim)


def steps_of(slot):
    first = (slot >= 9).astype(I32) + (slot >= 18).astype(I32)
    rest = slot - 9 * first
    second = (rest >= 3).astype(I32) + (rest >= 6).astype(I32)
    return first, second, rest - 3 * second


def half_rows(ref, base, half):
    return [ref[pl.ds(base + m * 2 * BLOCKS + half, BLOCKS, stride=2), :] for m in range(3)]


def message_kernel(count, raw, cells, pairs, out):
    out[:STATE, :] = raw[...]
    cell_row = jnp.concatenate([cells[...], jnp.zeros((1, LANES - BLOCKS), I32)], axis=1)
    cell_row = cell_row.astype(F32)
    blank = jnp.zeros((1, LANES - CAP), I32)
    listing = [jnp.concatenate([pairs[m], blank], axis=1) for m in range(3)]
    step_x, step_y, step_z = steps_of(listing[1])
    back_x, back_y, back_z = [jnp.where(s == 0, 1, 0) for s in (step_x, step_y, step_z)]
    key = back_x + 2 * back_y + 8 * back_z + jnp.where(step_z == 2, 4, 0)
    row_lane = iota((1, LANES), 1)
    key = jnp.where(row_lane < count[0], key, KINDS).astype(F32)
    wide_lane, wide_sub = iota((LANES, LANES), 1), iota((LANES, LANES), 0)
    key_down = jnp.sum(jnp.where(wide_lane == wide_sub, key, 0.0), axis=1, keepdims=True)
    starts = jnp.sum((key_down < wide_lane.astype(F32)).astype(F32), axis=0, keepdims=True)
    ahead = (key < key_down) | ((key == key_down) & (wide_lane < wide_sub))
    rank_down = jnp.sum(ahead.astype(F32), axis=1, keepdims=True)
    place = (rank_down == wide_lane.astype(F32)).astype(BF16)
    listing = [row.astype(F32) for row in listing] + [jnp.zeros((5, LANES), F32)]
    padded = jnp.concatenate(listing, axis=0).astype(BF16)
    order = jnp.dot(padded, place, preferred_element_type=F32)
    out[STATE:, :] = jnp.concatenate(
        [order[:3], starts, cell_row, jnp.zeros((3, LANES), F32)], axis=0
    )


def source_kernel(tree, message, far):
    sums = [jnp.zeros((BLOCKS, 1), F32)] * 6
    for half in range(2):
        moments = moment_of(half_rows(message, PART, half), half_rows(message, 2 * PART, half))
        sums = [a + jnp.sum(m, axis=1, keepdims=True) for a, m in zip(sums, moments)]
    lane, sub = iota((BLOCKS, LANES), 1), iota((BLOCKS, LANES), 0)
    cell_row = message[STATE + 4 : STATE + 5, :]
    cell = jnp.sum(jnp.where(lane == sub, cell_row, 0.0), axis=1, keepdims=True)
    chosen = cell == lane.astype(F32)
    rows = [jnp.sum(jnp.where(chosen, v, 0.0), axis=0, keepdims=True) for v in sums]
    rows.append(jnp.full((1, LANES), tree[0].astype(F32)))
    rows.append(jnp.zeros((1, LANES), F32))
    far[...] = jnp.concatenate(rows, axis=0)


def column(values):
    row = iota((8, 1), 0)
    out = jnp.zeros((8, 1), F32)
    for index, value in enumerate(values):
        if value:
            out = jnp.where(row == index, value, out)
    return out


def features(moment, y):
    first = [moment * v for v in y]
    second = [
        first[0] * y[0],
        first[1] * y[1],
        first[2] * y[2],
        first[1] * y[2],
        first[0] * y[2],
        first[0] * y[1],
    ]
    return halves(jnp.concatenate([moment] + first + second, axis=0))


def contract(sums, x):
    s0, s1, s2, s3, xx, yy, zz, yz, xz, xy = [sums[8 * i : 8 * i + 8] for i in range(10)]
    ux, uy, uz = s1 - x[0] * s0, s2 - x[1] * s0, s3 - x[2] * s0
    xx = xx - x[0] * (s1 + ux)
    yy = yy - x[1] * (s2 + uy)
    zz = zz - x[2] * (s3 + uz)
    yz = yz - x[1] * s3 - x[2] * uy
    xz = xz - x[0] * s3 - x[2] * ux
    xy = xy - x[0] * s2 - x[1] * ux
    row = iota((8, 1), 0)

    def pick(*terms):
        out = 0.0
        for group, at in terms:
            out = jnp.where(row == at, group, out)
        return out

    def move(value, by):
        return pltpu.roll(value, by % 8, 0)

    out = (
        CORE * s0
        + xx * column([-2, 1, 1, 1, -0.5, -0.5])
        + yy * column([1, -2, 1, -0.5, 1, -0.5])
        + zz * column([1, 1, -2, -0.5, -0.5, 1])
    )
    edge = pick((yz, 3), (xz, 4), (xy, 5))
    out += -3.0 * (
        move(jnp.where((row == 4) | (row == 5), edge, 0.0), -4)
        + move(jnp.where(row == 5, edge, 0.0), -5)
        + move(jnp.where((row == 3) | (row == 4), edge, 0.0), -2)
        + move(jnp.where(row == 3, edge, 0.0), -1)
    )
    out += -1.5 * (
        move(pick((xz, 5)), -2)
        + move(pick((xy, 4), (yz, 5)), -1)
        + move(pick((yz, 2), (xy, 3), (yz, 4)), 1)
        + move(pick((yz, 1), (xz, 2), (xz, 3)), 2)
        + move(pick((xz, 0), (xy, 1)), 4)
        + move(pick((xy, 0)), 5)
    )
    return out


NT = (((1,), (1,)), ((), ()))
NN = (((1,), (0,)), ((), ()))


def weights(x, y, apart):
    row = iota((8, 1), 0)
    xs = [x[c] + apart[c] for c in range(3)]
    norm_x = xs[0] * xs[0] + xs[1] * xs[1] + xs[2] * xs[2] + CORE
    norm_y = y[0] * y[0] + y[1] * y[1] + y[2] * y[2]
    left, right = jnp.where(row == 4, 1.0, 0.0), jnp.where(row == 3, 1.0, 0.0)
    for index in range(3):
        left = jnp.where(row == index, -2.0 * xs[index], left)
        right = jnp.where(row == index, y[index], right)
    left = jnp.where(row == 3, norm_x, left)
    right = jnp.where(row == 4, norm_y, right)
    l1, l2, l3 = thirds(left)
    r1, r2, r3 = thirds(right)
    square = lax.dot_general(
        jnp.concatenate([l1, l1, l2, l2, l1, l3], axis=0),
        jnp.concatenate([r1, r2, r1, r2, r3, r1], axis=0),
        (((0,), (0,)), ((), ())),
        preferred_element_type=F32,
    )
    inverse = lax.rsqrt(square)
    second = inverse * inverse
    return halves(second * second * inverse)


def apply(moment, at, high, low, dims):
    f_high, f_low = features(moment, at)
    count = f_high.shape[0]
    both = lax.dot_general(
        jnp.concatenate([f_high, f_low], axis=0), high, dims, preferred_element_type=F32
    )
    rest = lax.dot_general(f_high, low, dims, preferred_element_type=F32)
    return both[:count] + both[count:] + rest


def rows_of(ref, at):
    return jnp.concatenate([ref[0, at, :], ref[1, at, :]], axis=1)


def tile(block):
    return pl.ds(pl.multiple_of(block * 8, 8), 8)


def fill(refs, moments, offsets):
    for index, ref in enumerate(refs):

        def one(domain, carry, index=index, ref=ref):
            for half in range(2):
                x, b, l = [half_rows(ref, domain * ROWS + part * PART, half) for part in range(3)]
                zero = jnp.zeros((BLOCKS, LANES), F32)
                base = (4 * index + domain) * BLOCKS * 8
                for target, values in ((moments, moment_of(b, l) + [zero, zero]), (offsets, x)):
                    for member, value in enumerate(values):
                        target[half, pl.ds(base + member, BLOCKS, stride=8), :] = value
            return carry

        lax.fori_loop(0, 4, one, 0)


def finish(ref, arrays, far, shift, out):
    lane, sub = iota((BLOCKS, LANES), 1), iota((BLOCKS, LANES), 0)
    for domain in range(4):
        base = domain * ROWS
        cells = ref[base + STATE + 4 : base + STATE + 5, :]
        cell = jnp.sum(jnp.where(lane == sub, cells, 0.0), axis=1, keepdims=True)
        chosen = cell + float((shift + domain) * 8) == lane.astype(F32)
        extra = [jnp.sum(jnp.where(chosen, v, 0.0), axis=1, keepdims=True) for v in far]
        for half in range(2):
            b = half_rows(ref, base + PART, half)
            l = half_rows(ref, base + 2 * PART, half)
            total = extra
            for stress, first in arrays:
                start = (first + domain) * BLOCKS * 8
                total = [
                    v + stress[half, pl.ds(start + m, BLOCKS, stride=8), :]
                    for m, v in enumerate(total)
                ]
            for member, value in enumerate(force_of(total, b, l)):
                at = pl.ds(domain * PART + member * 2 * BLOCKS + half, BLOCKS, stride=2)
                out[at, :] = value


def offsets_of(offsets, block):
    out = []
    for member in range(3):
        at = pl.ds(block * 8 + member, 1)
        parts = [jnp.broadcast_to(offsets[h, at, :], (8, LANES)) for h in range(2)]
        out.append(jnp.concatenate(parts, axis=1))
    return out


def all_pairs(ints, groups, todo, moments, offsets, stress, high, low):
    total = jnp.int32(0)
    for kind, domain in groups:
        start, end = ints[domain * 8 + 3, kind], ints[domain * 8 + 3, kind + 1]

        def put(k, carry, domain=domain, start=start, total=total):
            todo[total + k - start] = domain * 64 + k
            return carry

        lax.fori_loop(start, end, put, 0)
        total = total + (end - start)
    spare = stress.shape[1] // 8 - 1

    def find(index):
        live = index < total
        item = todo[jnp.where(live, index, 0)]
        domain, k = item >> 6, item & 63
        first = ints[domain * 8, k]
        slot = ints[domain * 8 + 1, k]
        second = ints[domain * 8 + 2, k]
        step_x = (slot * 57) >> 9
        rest = slot - 9 * step_x
        step_y = (rest * 11) >> 5
        step_z = rest - 3 * step_y
        steps = [step_x - 1, step_y - 1, step_z - 1]
        other = domain + steps[0] + 2 * steps[1] + 4 * steps[2]
        cell_i, cell_j = ints[domain * 8 + 4, first], ints[other * 8 + 4, second]
        apart = []
        for member in range(3):
            bit = 2 - member
            gap = ((cell_i >> bit) & 1) - ((cell_j >> bit) & 1) - 2 * steps[member]
            apart.append(0.5 * gap.astype(F32))
        i, j = domain * BLOCKS + first, other * BLOCKS + second
        return i, j, jnp.where(live, i, spare), jnp.where(live, j, spare), apart

    def work(base, count):
        found = [find(base + index) for index in range(count)]
        for index, (i, j, _, _, apart) in enumerate(found):
            parts = weights(offsets_of(offsets, i), offsets_of(offsets, j), apart)
            high[index], low[index] = parts
        for index, (i, j, to_i, to_j, apart) in enumerate(found):
            x, y = offsets_of(offsets, i), offsets_of(offsets, j)
            xs = [x[c] + apart[c] for c in range(3)]
            ys = [y[c] - apart[c] for c in range(3)]
            on_i = apply(rows_of(moments, tile(j)), y, high[index], low[index], NT)
            on_j = apply(rows_of(moments, tile(i)), x, high[index], low[index], NN)
            for to, value in ((to_i, contract(on_i, xs)), (to_j, contract(on_j, ys))):
                stress[0, tile(to), :] += value[:, :LANES]
                stress[1, tile(to), :] += value[:, LANES:]

    whole, rest = total >> 3, total & 7
    rounds = whole + (rest > FEW).astype(I32)

    def many(turn, carry):
        work(turn * MANY, MANY)
        return carry

    def few(turn, carry):
        work(whole * MANY, FEW)
        return carry

    lax.fori_loop(0, rounds, many, 0)
    lax.fori_loop(0, ((rest > 0) & (rest <= FEW)).astype(I32), few, 0)


def pair_kernel(groups, parts, ints, *refs):
    states = refs[:parts]
    stress, moments, offsets, high, low, todo = refs[parts:]
    fill(states, moments, offsets)
    stress[...] = jnp.zeros_like(stress)
    all_pairs(ints, groups, todo, moments, offsets, stress, high, low)


def beyond_kernel(beyond, crossing, sources, out):
    finish(beyond, [(crossing, 4)], far_field(sources[...]), 4, out)


def near_kernel(near, inner, crossing, sources, out):
    finish(near, [(inner, 0), (crossing, 0)], far_field(sources[...]), 0, out)


def far_field(sources):
    row, lane = iota((64, LANES), 0), iota((64, LANES), 1)
    steps = []
    for member, size in enumerate((4, 4, 8)):
        place = 2 * ((lane >> (5, 6, 3)[member]) & 1)
        if member == 2:
            place = place + 4 * ((lane >> 4) & 1)
        step = place - ((row >> (3 + member)) & 1)
        steps.append(jnp.where(step > size // 2, step - size, step))
    most = functools.reduce(jnp.maximum, [jnp.abs(s) for s in steps])
    mask = (most > 1).astype(F32)
    tree = sources[6:7]
    r = []
    for member in range(3):
        bit = 2 - member
        at = 0.25 + 0.5 * ((row >> bit) & 1).astype(F32)
        own = 0.25 + 0.5 * ((lane >> bit) & 1).astype(F32)
        r.append(at - (jnp.where(tree == 1.0, own, 0.5) + steps[member].astype(F32)))
    xx, yy, zz, yz, xz, xy = [sources[m : m + 1] * mask for m in range(6)]
    inverse = lax.rsqrt(r[0] * r[0] + r[1] * r[1] + r[2] * r[2] + CORE)
    cubed = inverse * inverse * inverse
    weight = 3.0 * cubed * inverse * inverse
    ax = xx * r[0] + xy * r[1] + xz * r[2]
    ay = xy * r[0] + yy * r[1] + yz * r[2]
    az = xz * r[0] + yz * r[1] + zz * r[2]
    stress = [
        xx * cubed - weight * ax * r[0],
        yy * cubed - weight * ay * r[1],
        zz * cubed - weight * az * r[2],
        yz * cubed - 0.5 * weight * (ay * r[2] + az * r[1]),
        xz * cubed - 0.5 * weight * (ax * r[2] + az * r[0]),
        xy * cubed - 0.5 * weight * (ax * r[1] + ay * r[0]),
    ]
    out = []
    for value in stress:
        total = jnp.sum(value, axis=1, keepdims=True)
        out.append(jnp.sum(jnp.where(row == lane, total, 0.0), axis=0, keepdims=True))
    return out


def in_vmem(count):
    return [pl.BlockSpec(memory_space=pltpu.VMEM)] * count


def in_smem(count):
    return [pl.BlockSpec(memory_space=pltpu.SMEM)] * count


PARAMS = pltpu.CompilerParams(vmem_limit_bytes=VMEM_LIMIT)


def make_message(count, raw, cells, pairs):
    return pl.pallas_call(
        message_kernel,
        out_shape=jax.ShapeDtypeStruct((ROWS, LANES), F32),
        in_specs=in_smem(1) + in_vmem(3),
        out_specs=in_vmem(1)[0],
        compiler_params=PARAMS,
    )(count, raw, cells, pairs)


def make_source(tree, message):
    return pl.pallas_call(
        source_kernel,
        out_shape=jax.ShapeDtypeStruct((8, LANES), F32),
        in_specs=in_smem(1) + in_vmem(1),
        out_specs=in_vmem(1)[0],
        compiler_params=PARAMS,
    )(tree, message)


FORCES = jax.ShapeDtypeStruct((4 * PART, LANES), F32)
WORK = [pltpu.VMEM((MANY, WIDTH, WIDTH), BF16)] * 2 + [pltpu.SMEM((8 * CAP + 8,), I32)]


def pair_stress(groups, states):
    ints = [v.reshape(4, ROWS, LANES)[:, STATE:].reshape(-1, LANES) for v in states]
    blocks = 4 * len(states) * BLOCKS
    tiles = pltpu.VMEM((2, blocks * 8, LANES), F32)
    return pl.pallas_call(
        functools.partial(pair_kernel, groups, len(states)),
        out_shape=jax.ShapeDtypeStruct((2, (blocks + 1) * 8, LANES), F32),
        in_specs=in_smem(1) + in_vmem(len(states)),
        out_specs=in_vmem(1)[0],
        scratch_shapes=[tiles, tiles] + WORK,
        compiler_params=PARAMS,
        cost_estimate=pl.CostEstimate(flops=10**9, bytes_accessed=10**6, transcendentals=10**6),
    )(jnp.concatenate(ints).astype(I32), *states)


def forces(kernel, *arrays):
    return pl.pallas_call(
        kernel,
        out_shape=FORCES,
        in_specs=in_vmem(len(arrays)),
        out_specs=in_vmem(1)[0],
        compiler_params=PARAMS,
    )(*arrays)


def from_ahead(x, axis, by):
    size = lax.axis_size(axis)
    return lax.ppermute(x, axis, [(i, (i - by) % size) for i in range(size)])


def to_ahead(x, axis):
    size = lax.axis_size(axis)
    return lax.ppermute(x, axis, [(i, (i + 1) % size) for i in range(size)])


def grown(sources, axis, by):
    return jnp.concatenate([sources, from_ahead(sources, axis, by)], axis=1)


def shards(offsets, burgers, segvec, block_cell, tree_level, pair_count, pair_list):
    raw = jnp.concatenate([v.reshape(PART, LANES) for v in (offsets, burgers, segvec)])
    message = make_message(
        pair_count, raw, block_cell.reshape(1, BLOCKS), pair_list.reshape(3, 1, CAP)
    )
    sources = make_source(tree_level, message)[:, :8]
    ahead = from_ahead(message, "gx", 1)
    ahead, sources = lax.optimization_barrier((ahead, grown(sources, "gz", 2)))
    line = jnp.concatenate([message, ahead])
    ahead = from_ahead(line, "gy", 1)
    ahead, sources = lax.optimization_barrier((ahead, grown(sources, "gz", 4)))
    near = jnp.concatenate([line, ahead])
    beyond = from_ahead(near, "gz", 1)
    inner = pair_stress([(d, d) for d in range(4)], [near])
    sources = grown(sources, "gx", 2)
    beyond, inner, sources = lax.optimization_barrier((beyond, inner, sources))
    groups = [(4 + d, d) for d in range(4)] + [(8 + d, 4 + d) for d in range(4)]
    crossing = pair_stress(groups, [near, beyond])
    sources = grown(sources, "gy", 2)
    force = to_ahead(forces(beyond_kernel, beyond, crossing, sources), "gz")
    force = force + forces(near_kernel, near, inner, crossing, sources)
    force = force[: 2 * PART] + to_ahead(force[2 * PART :], "gy")
    force = force[:PART] + to_ahead(force[PART:], "gx")
    return force.reshape(offsets.shape)


def solution(mesh):
    in_specs = (
        P("gx", "gy", "gz", None, None),
        P("gx", "gy", "gz", None, None),
        P("gx", "gy", "gz", None, None),
        P("gx", "gy", "gz", None),
        P(("gx", "gy", "gz")),
        P(("gx", "gy", "gz")),
        P("gx", "gy", "gz", None, None),
    )
    out_specs = P("gx", "gy", "gz", None, None)
    return jax.shard_map(shards, mesh=mesh, in_specs=in_specs, out_specs=out_specs, check_vma=False)
```

```python
import functools

import jax
import jax.numpy as jnp
from jax import lax
from jax.experimental import pallas as pl
from jax.experimental.pallas import tpu as pltpu
from jax.sharding import PartitionSpec as P

F32, BF16, I32 = jnp.float32, jnp.bfloat16, jnp.int32
CORE = 0.04
LANES = 128
WIDTH = 256
BLOCKS = 16
CAP = 48
PART = 3 * 2 * BLOCKS
STATE = 3 * PART
ROWS = STATE + 8
KINDS = 12
MANY, FEW = 8, 4
VMEM_LIMIT = 48 * 1024 * 1024


def halves(x):
    high = x.astype(BF16)
    return high, (x - high.astype(F32)).astype(BF16)


def thirds(x):
    high = x.astype(BF16)
    rest = x - high.astype(F32)
    middle = rest.astype(BF16)
    return high, middle, (rest - middle.astype(F32)).astype(BF16)


def moment_of(b, l):
    return [
        b[0] * l[0],
        b[1] * l[1],
        b[2] * l[2],
        0.5 * (b[1] * l[2] + b[2] * l[1]),
        0.5 * (b[0] * l[2] + b[2] * l[0]),
        0.5 * (b[0] * l[1] + b[1] * l[0]),
    ]


def force_of(stress, b, l):
    xx, yy, zz, yz, xz, xy = stress
    px = xx * b[0] + xy * b[1] + xz * b[2]
    py = xy * b[0] + yy * b[1] + yz * b[2]
    pz = xz * b[0] + yz * b[1] + zz * b[2]
    return [py * l[2] - pz * l[1], pz * l[0] - px * l[2], px * l[1] - py * l[0]]


def iota(shape, dim):
    return lax.broadcasted_iota(I32, shape, dim)


def steps_of(slot):
    first = (slot >= 9).astype(I32) + (slot >= 18).astype(I32)
    rest = slot - 9 * first
    second = (rest >= 3).astype(I32) + (rest >= 6).astype(I32)
    return first, second, rest - 3 * second


def half_rows(ref, base, half):
    return [ref[pl.ds(base + m * 2 * BLOCKS + half, BLOCKS, stride=2), :] for m in range(3)]


def message_kernel(count, raw, notes, out):
    out[:STATE, :] = raw[...]
    cell_row = notes[3:4, :].astype(F32)
    listing = [notes[m : m + 1, :] for m in range(3)]
    step_x, step_y, step_z = steps_of(listing[1])
    back_x, back_y, back_z = [jnp.where(s == 0, 1, 0) for s in (step_x, step_y, step_z)]
    key = back_x + 2 * back_y + 8 * back_z + jnp.where(step_z == 2, 4, 0)
    row_lane = iota((1, LANES), 1)
    key = jnp.where(row_lane < count[0], key, KINDS).astype(F32)
    wide_lane, wide_sub = iota((LANES, LANES), 1), iota((LANES, LANES), 0)
    key_down = jnp.sum(jnp.where(wide_lane == wide_sub, key, 0.0), axis=1, keepdims=True)
    starts = jnp.sum((key_down < wide_lane.astype(F32)).astype(F32), axis=0, keepdims=True)
    ahead = (key < key_down) | ((key == key_down) & (wide_lane < wide_sub))
    rank_down = jnp.sum(ahead.astype(F32), axis=1, keepdims=True)
    place = (rank_down == wide_lane.astype(F32)).astype(BF16)
    listing = [row.astype(F32) for row in listing] + [jnp.zeros((5, LANES), F32)]
    padded = jnp.concatenate(listing, axis=0).astype(BF16)
    order = jnp.dot(padded, place, preferred_element_type=F32)
    out[STATE:, :] = jnp.concatenate(
        [order[:3], starts, cell_row, jnp.zeros((3, LANES), F32)], axis=0
    )


def source_kernel(tree, message, far):
    sums = [jnp.zeros((BLOCKS, 1), F32)] * 6
    for half in range(2):
        moments = moment_of(half_rows(message, PART, half), half_rows(message, 2 * PART, half))
        sums = [a + jnp.sum(m, axis=1, keepdims=True) for a, m in zip(sums, moments)]
    lane, sub = iota((BLOCKS, LANES), 1), iota((BLOCKS, LANES), 0)
    cell_row = message[STATE + 4 : STATE + 5, :]
    cell = jnp.sum(jnp.where(lane == sub, cell_row, 0.0), axis=1, keepdims=True)
    chosen = cell == lane.astype(F32)
    rows = [jnp.sum(jnp.where(chosen, v, 0.0), axis=0, keepdims=True) for v in sums]
    rows.append(jnp.full((1, LANES), tree[0].astype(F32)))
    rows.append(jnp.zeros((1, LANES), F32))
    far[...] = jnp.concatenate(rows, axis=0)


def column(values):
    row = iota((8, 1), 0)
    out = jnp.zeros((8, 1), F32)
    for index, value in enumerate(values):
        if value:
            out = jnp.where(row == index, value, out)
    return out


def features(moment, y):
    first = [moment * v for v in y]
    second = [
        first[0] * y[0],
        first[1] * y[1],
        first[2] * y[2],
        first[1] * y[2],
        first[0] * y[2],
        first[0] * y[1],
    ]
    return halves(jnp.concatenate([moment] + first + second, axis=0))


def contract(sums, x):
    s0, s1, s2, s3, xx, yy, zz, yz, xz, xy = [sums[8 * i : 8 * i + 8] for i in range(10)]
    ux, uy, uz = s1 - x[0] * s0, s2 - x[1] * s0, s3 - x[2] * s0
    xx = xx - x[0] * (s1 + ux)
    yy = yy - x[1] * (s2 + uy)
    zz = zz - x[2] * (s3 + uz)
    yz = yz - x[1] * s3 - x[2] * uy
    xz = xz - x[0] * s3 - x[2] * ux
    xy = xy - x[0] * s2 - x[1] * ux
    row = iota((8, 1), 0)

    def pick(*terms):
        out = 0.0
        for group, at in terms:
            out = jnp.where(row == at, group, out)
        return out

    def move(value, by):
        return pltpu.roll(value, by % 8, 0)

    out = (
        CORE * s0
        + xx * column([-2, 1, 1, 1, -0.5, -0.5])
        + yy * column([1, -2, 1, -0.5, 1, -0.5])
        + zz * column([1, 1, -2, -0.5, -0.5, 1])
    )
    edge = pick((yz, 3), (xz, 4), (xy, 5))
    out += -3.0 * (
        move(jnp.where((row == 4) | (row == 5), edge, 0.0), -4)
        + move(jnp.where(row == 5, edge, 0.0), -5)
        + move(jnp.where((row == 3) | (row == 4), edge, 0.0), -2)
        + move(jnp.where(row == 3, edge, 0.0), -1)
    )
    out += -1.5 * (
        move(pick((xz, 5)), -2)
        + move(pick((xy, 4), (yz, 5)), -1)
        + move(pick((yz, 2), (xy, 3), (yz, 4)), 1)
        + move(pick((yz, 1), (xz, 2), (xz, 3)), 2)
        + move(pick((xz, 0), (xy, 1)), 4)
        + move(pick((xy, 0)), 5)
    )
    return out


NT = (((1,), (1,)), ((), ()))
NN = (((1,), (0,)), ((), ()))


def weights(x, y, apart):
    row = iota((8, 1), 0)
    xs = [x[c] + apart[c] for c in range(3)]
    norm_x = xs[0] * xs[0] + xs[1] * xs[1] + xs[2] * xs[2] + CORE
    norm_y = y[0] * y[0] + y[1] * y[1] + y[2] * y[2]
    left, right = jnp.where(row == 4, 1.0, 0.0), jnp.where(row == 3, 1.0, 0.0)
    for index in range(3):
        left = jnp.where(row == index, -2.0 * xs[index], left)
        right = jnp.where(row == index, y[index], right)
    left = jnp.where(row == 3, norm_x, left)
    right = jnp.where(row == 4, norm_y, right)
    l1, l2, l3 = thirds(left)
    r1, r2, r3 = thirds(right)
    square = lax.dot_general(
        jnp.concatenate([l1, l1, l2, l2, l1, l3], axis=0),
        jnp.concatenate([r1, r2, r1, r2, r3, r1], axis=0),
        (((0,), (0,)), ((), ())),
        preferred_element_type=F32,
    )
    inverse = lax.rsqrt(square)
    second = inverse * inverse
    return halves(second * second * inverse)


def apply(moment, at, high, low, dims):
    f_high, f_low = features(moment, at)
    count = f_high.shape[0]
    both = lax.dot_general(
        jnp.concatenate([f_high, f_low], axis=0), high, dims, preferred_element_type=F32
    )
    rest = lax.dot_general(f_high, low, dims, preferred_element_type=F32)
    return both[:count] + both[count:] + rest


def rows_of(ref, at):
    return jnp.concatenate([ref[0, at, :], ref[1, at, :]], axis=1)


def tile(block):
    return pl.ds(pl.multiple_of(block * 8, 8), 8)


def fill(refs, moments, offsets):
    for index, ref in enumerate(refs):

        def one(domain, carry, index=index, ref=ref):
            for half in range(2):
                x, b, l = [half_rows(ref, domain * ROWS + part * PART, half) for part in range(3)]
                zero = jnp.zeros((BLOCKS, LANES), F32)
                base = (4 * index + domain) * BLOCKS * 8
                for target, values in ((moments, moment_of(b, l) + [zero, zero]), (offsets, x)):
                    for member, value in enumerate(values):
                        target[half, pl.ds(base + member, BLOCKS, stride=8), :] = value
            return carry

        lax.fori_loop(0, 4, one, 0)


def finish(ref, arrays, far, shift, out):
    lane, sub = iota((BLOCKS, LANES), 1), iota((BLOCKS, LANES), 0)
    for domain in range(4):
        base = domain * ROWS
        cells = ref[base + STATE + 4 : base + STATE + 5, :]
        cell = jnp.sum(jnp.where(lane == sub, cells, 0.0), axis=1, keepdims=True)
        chosen = cell + float((shift + domain) * 8) == lane.astype(F32)
        extra = [jnp.sum(jnp.where(chosen, v, 0.0), axis=1, keepdims=True) for v in far]
        for half in range(2):
            b = half_rows(ref, base + PART, half)
            l = half_rows(ref, base + 2 * PART, half)
            total = extra
            for stress, first in arrays:
                start = (first + domain) * BLOCKS * 8
                total = [
                    v + stress[half, pl.ds(start + m, BLOCKS, stride=8), :]
                    for m, v in enumerate(total)
                ]
            for member, value in enumerate(force_of(total, b, l)):
                at = pl.ds(domain * PART + member * 2 * BLOCKS + half, BLOCKS, stride=2)
                out[at, :] = value


def offsets_of(offsets, block):
    out = []
    for member in range(3):
        at = pl.ds(block * 8 + member, 1)
        parts = [jnp.broadcast_to(offsets[h, at, :], (8, LANES)) for h in range(2)]
        out.append(jnp.concatenate(parts, axis=1))
    return out


def all_pairs(ints, groups, todo, moments, offsets, stress, high, low):
    total = jnp.int32(0)
    for kind, domain in groups:
        start, end = ints[domain * 8 + 3, kind], ints[domain * 8 + 3, kind + 1]

        def put(k, carry, domain=domain, start=start, total=total):
            todo[total + k - start] = domain * 64 + k
            return carry

        lax.fori_loop(start, end, put, 0)
        total = total + (end - start)
    spare = stress.shape[1] // 8 - 1

    def find(index):
        live = index < total
        item = todo[jnp.where(live, index, 0)]
        domain, k = item >> 6, item & 63
        first = ints[domain * 8, k]
        slot = ints[domain * 8 + 1, k]
        second = ints[domain * 8 + 2, k]
        step_x = (slot * 57) >> 9
        rest = slot - 9 * step_x
        step_y = (rest * 11) >> 5
        step_z = rest - 3 * step_y
        steps = [step_x - 1, step_y - 1, step_z - 1]
        other = domain + steps[0] + 2 * steps[1] + 4 * steps[2]
        cell_i, cell_j = ints[domain * 8 + 4, first], ints[other * 8 + 4, second]
        apart = []
        for member in range(3):
            bit = 2 - member
            gap = ((cell_i >> bit) & 1) - ((cell_j >> bit) & 1) - 2 * steps[member]
            apart.append(0.5 * gap.astype(F32))
        i, j = domain * BLOCKS + first, other * BLOCKS + second
        return i, j, jnp.where(live, i, spare), jnp.where(live, j, spare), apart

    def work(base, count):
        found = [find(base + index) for index in range(count)]
        for index, (i, j, _, _, apart) in enumerate(found):
            parts = weights(offsets_of(offsets, i), offsets_of(offsets, j), apart)
            high[index], low[index] = parts
        for index, (i, j, to_i, to_j, apart) in enumerate(found):
            x, y = offsets_of(offsets, i), offsets_of(offsets, j)
            xs = [x[c] + apart[c] for c in range(3)]
            ys = [y[c] - apart[c] for c in range(3)]
            on_i = apply(rows_of(moments, tile(j)), y, high[index], low[index], NT)
            on_j = apply(rows_of(moments, tile(i)), x, high[index], low[index], NN)
            for to, value in ((to_i, contract(on_i, xs)), (to_j, contract(on_j, ys))):
                stress[0, tile(to), :] += value[:, :LANES]
                stress[1, tile(to), :] += value[:, LANES:]

    whole, rest = total >> 3, total & 7
    rounds = whole + (rest > FEW).astype(I32)

    def many(turn, carry):
        work(turn * MANY, MANY)
        return carry

    def few(turn, carry):
        work(whole * MANY, FEW)
        return carry

    lax.fori_loop(0, rounds, many, 0)
    lax.fori_loop(0, ((rest > 0) & (rest <= FEW)).astype(I32), few, 0)


def pair_kernel(groups, parts, ints, *refs):
    states = refs[:parts]
    stress, moments, offsets, high, low, todo = refs[parts:]
    fill(states, moments, offsets)
    stress[...] = jnp.zeros_like(stress)
    all_pairs(ints, groups, todo, moments, offsets, stress, high, low)


def beyond_kernel(beyond, crossing, sources, out):
    finish(beyond, [(crossing, 4)], far_field(sources[...]), 4, out)


def near_kernel(near, inner, crossing, sources, out):
    finish(near, [(inner, 0), (crossing, 0)], far_field(sources[...]), 0, out)


def far_field(sources):
    row, lane = iota((64, LANES), 0), iota((64, LANES), 1)
    steps = []
    for member, size in enumerate((4, 4, 8)):
        place = 2 * ((lane >> (4, 5, 3)[member]) & 1)
        if member == 2:
            place = place + 4 * ((lane >> 6) & 1)
        step = place - ((row >> (3 + member)) & 1)
        steps.append(jnp.where(step > size // 2, step - size, step))
    most = functools.reduce(jnp.maximum, [jnp.abs(s) for s in steps])
    mask = (most > 1).astype(F32)
    tree = sources[6:7]
    r = []
    for member in range(3):
        bit = 2 - member
        at = 0.25 + 0.5 * ((row >> bit) & 1).astype(F32)
        own = 0.25 + 0.5 * ((lane >> bit) & 1).astype(F32)
        r.append(at - (jnp.where(tree == 1.0, own, 0.5) + steps[member].astype(F32)))
    xx, yy, zz, yz, xz, xy = [sources[m : m + 1] * mask for m in range(6)]
    inverse = lax.rsqrt(r[0] * r[0] + r[1] * r[1] + r[2] * r[2] + CORE)
    cubed = inverse * inverse * inverse
    weight = 3.0 * cubed * inverse * inverse
    ax = xx * r[0] + xy * r[1] + xz * r[2]
    ay = xy * r[0] + yy * r[1] + yz * r[2]
    az = xz * r[0] + yz * r[1] + zz * r[2]
    stress = [
        xx * cubed - weight * ax * r[0],
        yy * cubed - weight * ay * r[1],
        zz * cubed - weight * az * r[2],
        yz * cubed - 0.5 * weight * (ay * r[2] + az * r[1]),
        xz * cubed - 0.5 * weight * (ax * r[2] + az * r[0]),
        xy * cubed - 0.5 * weight * (ax * r[1] + ay * r[0]),
    ]
    out = []
    for value in stress:
        total = jnp.sum(value, axis=1, keepdims=True)
        out.append(jnp.sum(jnp.where(row == lane, total, 0.0), axis=0, keepdims=True))
    return out


def in_vmem(count):
    return [pl.BlockSpec(memory_space=pltpu.VMEM)] * count


def in_smem(count):
    return [pl.BlockSpec(memory_space=pltpu.SMEM)] * count


PARAMS = pltpu.CompilerParams(vmem_limit_bytes=VMEM_LIMIT)


def make_message(count, raw, notes):
    return pl.pallas_call(
        message_kernel,
        out_shape=jax.ShapeDtypeStruct((ROWS, LANES), F32),
        in_specs=in_smem(1) + in_vmem(2),
        out_specs=in_vmem(1)[0],
        compiler_params=PARAMS,
    )(count, raw, notes)


def make_source(tree, message):
    return pl.pallas_call(
        source_kernel,
        out_shape=jax.ShapeDtypeStruct((8, LANES), F32),
        in_specs=in_smem(1) + in_vmem(1),
        out_specs=in_vmem(1)[0],
        compiler_params=PARAMS,
    )(tree, message)


FORCES = jax.ShapeDtypeStruct((4 * PART, LANES), F32)
WORK = [pltpu.VMEM((MANY, WIDTH, WIDTH), BF16)] * 2 + [pltpu.SMEM((8 * CAP + 8,), I32)]


def pair_stress(groups, states):
    ints = [v.reshape(4, ROWS, LANES)[:, STATE:].reshape(-1, LANES) for v in states]
    blocks = 4 * len(states) * BLOCKS
    tiles = pltpu.VMEM((2, blocks * 8, LANES), F32)
    return pl.pallas_call(
        functools.partial(pair_kernel, groups, len(states)),
        out_shape=jax.ShapeDtypeStruct((2, (blocks + 1) * 8, LANES), F32),
        in_specs=in_smem(1) + in_vmem(len(states)),
        out_specs=in_vmem(1)[0],
        scratch_shapes=[tiles, tiles] + WORK,
        compiler_params=PARAMS,
        cost_estimate=pl.CostEstimate(flops=10**9, bytes_accessed=10**6, transcendentals=10**6),
    )(jnp.concatenate(ints).astype(I32), *states)


def forces(kernel, *arrays):
    return pl.pallas_call(
        kernel,
        out_shape=FORCES,
        in_specs=in_vmem(len(arrays)),
        out_specs=in_vmem(1)[0],
        compiler_params=PARAMS,
    )(*arrays)


def from_ahead(x, axis, by):
    size = lax.axis_size(axis)
    return lax.ppermute(x, axis, [(i, (i - by) % size) for i in range(size)])


def to_ahead(x, axis):
    size = lax.axis_size(axis)
    return lax.ppermute(x, axis, [(i, (i + 1) % size) for i in range(size)])


def grown(sources, axis, by):
    return jnp.concatenate([sources, from_ahead(sources, axis, by)], axis=1)


def shards(offsets, burgers, segvec, block_cell, tree_level, pair_count, pair_list):
    raw = jnp.concatenate([v.reshape(PART, LANES) for v in (offsets, burgers, segvec)])
    notes = [
        jnp.pad(pair_list.reshape(3, CAP), ((0, 0), (0, LANES - CAP))),
        jnp.pad(block_cell.reshape(1, BLOCKS), ((0, 0), (0, LANES - BLOCKS))),
    ]
    message = make_message(pair_count, raw, jnp.concatenate(notes))
    sources = make_source(tree_level, message)[:, :8]
    ahead = from_ahead(message, "gx", 1)
    ahead, sources = lax.optimization_barrier((ahead, grown(sources, "gz", 2)))
    line = jnp.concatenate([message, ahead])
    ahead = from_ahead(line, "gy", 1)
    ahead, sources = lax.optimization_barrier((ahead, grown(sources, "gx", 2)))
    near = jnp.concatenate([line, ahead])
    beyond = from_ahead(near, "gz", 1)
    inner = pair_stress([(d, d) for d in range(4)], [near])
    sources = grown(sources, "gy", 2)
    beyond, inner, sources = lax.optimization_barrier((beyond, inner, sources))
    groups = [(4 + d, d) for d in range(4)] + [(8 + d, 4 + d) for d in range(4)]
    crossing = pair_stress(groups, [near, beyond])
    sources = grown(sources, "gz", 4)
    force = to_ahead(forces(beyond_kernel, beyond, crossing, sources), "gz")
    force = force + forces(near_kernel, near, inner, crossing, sources)
    force = force[: 2 * PART] + to_ahead(force[2 * PART :], "gy")
    force = force[:PART] + to_ahead(force[PART:], "gx")
    return force.reshape(offsets.shape)


def solution(mesh):
    in_specs = (
        P("gx", "gy", "gz", None, None),
        P("gx", "gy", "gz", None, None),
        P("gx", "gy", "gz", None, None),
        P("gx", "gy", "gz", None),
        P(("gx", "gy", "gz")),
        P(("gx", "gy", "gz")),
        P("gx", "gy", "gz", None, None),
    )
    out_specs = P("gx", "gy", "gz", None, None)
    return jax.shard_map(shards, mesh=mesh, in_specs=in_specs, out_specs=out_specs, check_vma=False)
```

```python
import functools

import jax
import jax.numpy as jnp
from jax import lax
from jax.experimental import pallas as pl
from jax.experimental.pallas import tpu as pltpu
from jax.sharding import PartitionSpec as P

F32, BF16, I32 = jnp.float32, jnp.bfloat16, jnp.int32
CORE = 0.04
LANES = 128
WIDTH = 256
BLOCKS = 16
CAP = 48
PART = 3 * 2 * BLOCKS
STATE = 3 * PART
ROWS = STATE + 8
KINDS = 12
MANY, FEW = 8, 4
VMEM_LIMIT = 48 * 1024 * 1024


def halves(x):
    high = x.astype(BF16)
    return high, (x - high.astype(F32)).astype(BF16)


def thirds(x):
    high = x.astype(BF16)
    rest = x - high.astype(F32)
    middle = rest.astype(BF16)
    return high, middle, (rest - middle.astype(F32)).astype(BF16)


def moment_of(b, l):
    return [
        b[0] * l[0],
        b[1] * l[1],
        b[2] * l[2],
        0.5 * (b[1] * l[2] + b[2] * l[1]),
        0.5 * (b[0] * l[2] + b[2] * l[0]),
        0.5 * (b[0] * l[1] + b[1] * l[0]),
    ]


def force_of(stress, b, l):
    xx, yy, zz, yz, xz, xy = stress
    px = xx * b[0] + xy * b[1] + xz * b[2]
    py = xy * b[0] + yy * b[1] + yz * b[2]
    pz = xz * b[0] + yz * b[1] + zz * b[2]
    return [py * l[2] - pz * l[1], pz * l[0] - px * l[2], px * l[1] - py * l[0]]


def iota(shape, dim):
    return lax.broadcasted_iota(I32, shape, dim)


def steps_of(slot):
    first = (slot >= 9).astype(I32) + (slot >= 18).astype(I32)
    rest = slot - 9 * first
    second = (rest >= 3).astype(I32) + (rest >= 6).astype(I32)
    return first, second, rest - 3 * second


def half_rows(ref, base, half):
    return [ref[pl.ds(base + m * 2 * BLOCKS + half, BLOCKS, stride=2), :] for m in range(3)]


def message_kernel(count, raw, notes, out):
    out[:STATE, :] = raw[...]
    cell_row = notes[3:4, :].astype(F32)
    listing = [notes[m : m + 1, :] for m in range(3)]
    step_x, step_y, step_z = steps_of(listing[1])
    back_x, back_y, back_z = [jnp.where(s == 0, 1, 0) for s in (step_x, step_y, step_z)]
    key = back_x + 2 * back_y + 8 * back_z + jnp.where(step_z == 2, 4, 0)
    row_lane = iota((1, LANES), 1)
    key = jnp.where(row_lane < count[0], key, KINDS).astype(F32)
    wide_lane, wide_sub = iota((LANES, LANES), 1), iota((LANES, LANES), 0)
    key_down = jnp.sum(jnp.where(wide_lane == wide_sub, key, 0.0), axis=1, keepdims=True)
    starts = jnp.sum((key_down < wide_lane.astype(F32)).astype(F32), axis=0, keepdims=True)
    ahead = (key < key_down) | ((key == key_down) & (wide_lane < wide_sub))
    rank_down = jnp.sum(ahead.astype(F32), axis=1, keepdims=True)
    place = (rank_down == wide_lane.astype(F32)).astype(BF16)
    listing = [row.astype(F32) for row in listing] + [jnp.zeros((5, LANES), F32)]
    padded = jnp.concatenate(listing, axis=0).astype(BF16)
    order = jnp.dot(padded, place, preferred_element_type=F32)
    out[STATE:, :] = jnp.concatenate(
        [order[:3], starts, cell_row, jnp.zeros((3, LANES), F32)], axis=0
    )


def source_kernel(tree, message, far):
    sums = [jnp.zeros((BLOCKS, 1), F32)] * 6
    for half in range(2):
        moments = moment_of(half_rows(message, PART, half), half_rows(message, 2 * PART, half))
        sums = [a + jnp.sum(m, axis=1, keepdims=True) for a, m in zip(sums, moments)]
    lane, sub = iota((BLOCKS, LANES), 1), iota((BLOCKS, LANES), 0)
    cell_row = message[STATE + 4 : STATE + 5, :]
    cell = jnp.sum(jnp.where(lane == sub, cell_row, 0.0), axis=1, keepdims=True)
    chosen = cell == lane.astype(F32)
    rows = [jnp.sum(jnp.where(chosen, v, 0.0), axis=0, keepdims=True) for v in sums]
    rows.append(jnp.full((1, LANES), tree[0].astype(F32)))
    rows.append(jnp.zeros((1, LANES), F32))
    far[...] = jnp.concatenate(rows, axis=0)


def column(values):
    row = iota((8, 1), 0)
    out = jnp.zeros((8, 1), F32)
    for index, value in enumerate(values):
        if value:
            out = jnp.where(row == index, value, out)
    return out


def features(moment, y):
    first = [moment * v for v in y]
    second = [
        first[0] * y[0],
        first[1] * y[1],
        first[2] * y[2],
        first[1] * y[2],
        first[0] * y[2],
        first[0] * y[1],
    ]
    return halves(jnp.concatenate([moment] + first + second, axis=0))


def contract(sums, x):
    s0, s1, s2, s3, xx, yy, zz, yz, xz, xy = [sums[8 * i : 8 * i + 8] for i in range(10)]
    ux, uy, uz = s1 - x[0] * s0, s2 - x[1] * s0, s3 - x[2] * s0
    xx = xx - x[0] * (s1 + ux)
    yy = yy - x[1] * (s2 + uy)
    zz = zz - x[2] * (s3 + uz)
    yz = yz - x[1] * s3 - x[2] * uy
    xz = xz - x[0] * s3 - x[2] * ux
    xy = xy - x[0] * s2 - x[1] * ux
    row = iota((8, 1), 0)

    def pick(*terms):
        out = 0.0
        for group, at in terms:
            out = jnp.where(row == at, group, out)
        return out

    def move(value, by):
        return pltpu.roll(value, by % 8, 0)

    out = (
        CORE * s0
        + xx * column([-2, 1, 1, 1, -0.5, -0.5])
        + yy * column([1, -2, 1, -0.5, 1, -0.5])
        + zz * column([1, 1, -2, -0.5, -0.5, 1])
    )
    edge = pick((yz, 3), (xz, 4), (xy, 5))
    out += -3.0 * (
        move(jnp.where((row == 4) | (row == 5), edge, 0.0), -4)
        + move(jnp.where(row == 5, edge, 0.0), -5)
        + move(jnp.where((row == 3) | (row == 4), edge, 0.0), -2)
        + move(jnp.where(row == 3, edge, 0.0), -1)
    )
    out += -1.5 * (
        move(pick((xz, 5)), -2)
        + move(pick((xy, 4), (yz, 5)), -1)
        + move(pick((yz, 2), (xy, 3), (yz, 4)), 1)
        + move(pick((yz, 1), (xz, 2), (xz, 3)), 2)
        + move(pick((xz, 0), (xy, 1)), 4)
        + move(pick((xy, 0)), 5)
    )
    return out


NT = (((1,), (1,)), ((), ()))
NN = (((1,), (0,)), ((), ()))


def weights(x, y, apart):
    row = iota((8, 1), 0)
    xs = [x[c] + apart[c] for c in range(3)]
    norm_x = xs[0] * xs[0] + xs[1] * xs[1] + xs[2] * xs[2] + CORE
    norm_y = y[0] * y[0] + y[1] * y[1] + y[2] * y[2]
    left, right = jnp.where(row == 4, 1.0, 0.0), jnp.where(row == 3, 1.0, 0.0)
    for index in range(3):
        left = jnp.where(row == index, -2.0 * xs[index], left)
        right = jnp.where(row == index, y[index], right)
    left = jnp.where(row == 3, norm_x, left)
    right = jnp.where(row == 4, norm_y, right)
    l1, l2, l3 = thirds(left)
    r1, r2, r3 = thirds(right)
    square = lax.dot_general(
        jnp.concatenate([l1, l1, l2, l2, l1, l3], axis=0),
        jnp.concatenate([r1, r2, r1, r2, r3, r1], axis=0),
        (((0,), (0,)), ((), ())),
        preferred_element_type=F32,
    )
    inverse = lax.rsqrt(square)
    second = inverse * inverse
    return halves(second * second * inverse)


def apply(moment, at, high, low, dims):
    f_high, f_low = features(moment, at)
    count = f_high.shape[0]
    both = lax.dot_general(
        jnp.concatenate([f_high, f_low], axis=0), high, dims, preferred_element_type=F32
    )
    rest = lax.dot_general(f_high, low, dims, preferred_element_type=F32)
    return both[:count] + both[count:] + rest


def rows_of(ref, at):
    return jnp.concatenate([ref[0, at, :], ref[1, at, :]], axis=1)


def tile(block):
    return pl.ds(pl.multiple_of(block * 8, 8), 8)


def fill(refs, moments, offsets):
    for index, ref in enumerate(refs):

        def one(domain, carry, index=index, ref=ref):
            for half in range(2):
                x, b, l = [half_rows(ref, domain * ROWS + part * PART, half) for part in range(3)]
                zero = jnp.zeros((BLOCKS, LANES), F32)
                base = (4 * index + domain) * BLOCKS * 8
                for target, values in ((moments, moment_of(b, l) + [zero, zero]), (offsets, x)):
                    for member, value in enumerate(values):
                        target[half, pl.ds(base + member, BLOCKS, stride=8), :] = value
            return carry

        lax.fori_loop(0, 4, one, 0)


def finish(ref, arrays, far, shift, out):
    lane, sub = iota((BLOCKS, LANES), 1), iota((BLOCKS, LANES), 0)
    for domain in range(4):
        base = domain * ROWS
        cells = ref[base + STATE + 4 : base + STATE + 5, :]
        cell = jnp.sum(jnp.where(lane == sub, cells, 0.0), axis=1, keepdims=True)
        chosen = cell + float((shift + domain) * 8) == lane.astype(F32)
        extra = [jnp.sum(jnp.where(chosen, v, 0.0), axis=1, keepdims=True) for v in far]
        for half in range(2):
            b = half_rows(ref, base + PART, half)
            l = half_rows(ref, base + 2 * PART, half)
            total = extra
            for stress, first in arrays:
                start = (first + domain) * BLOCKS * 8
                total = [
                    v + stress[half, pl.ds(start + m, BLOCKS, stride=8), :]
                    for m, v in enumerate(total)
                ]
            for member, value in enumerate(force_of(total, b, l)):
                at = pl.ds(domain * PART + member * 2 * BLOCKS + half, BLOCKS, stride=2)
                out[at, :] = value


def offsets_of(offsets, block):
    out = []
    for member in range(3):
        at = pl.ds(block * 8 + member, 1)
        parts = [jnp.broadcast_to(offsets[h, at, :], (8, LANES)) for h in range(2)]
        out.append(jnp.concatenate(parts, axis=1))
    return out


def all_pairs(ints, groups, todo, moments, offsets, stress, high, low):
    total = jnp.int32(0)
    for kind, domain in groups:
        start, end = ints[domain * 8 + 3, kind], ints[domain * 8 + 3, kind + 1]

        def put(k, carry, domain=domain, start=start, total=total):
            todo[total + k - start] = domain * 64 + k
            return carry

        lax.fori_loop(start, end, put, 0)
        total = total + (end - start)
    spare = stress.shape[1] // 8 - 1

    def find(index):
        live = index < total
        item = todo[jnp.where(live, index, 0)]
        domain, k = item >> 6, item & 63
        first = ints[domain * 8, k]
        slot = ints[domain * 8 + 1, k]
        second = ints[domain * 8 + 2, k]
        step_x = (slot * 57) >> 9
        rest = slot - 9 * step_x
        step_y = (rest * 11) >> 5
        step_z = rest - 3 * step_y
        steps = [step_x - 1, step_y - 1, step_z - 1]
        other = domain + steps[0] + 2 * steps[1] + 4 * steps[2]
        cell_i, cell_j = ints[domain * 8 + 4, first], ints[other * 8 + 4, second]
        apart = []
        for member in range(3):
            bit = 2 - member
            gap = ((cell_i >> bit) & 1) - ((cell_j >> bit) & 1) - 2 * steps[member]
            apart.append(0.5 * gap.astype(F32))
        i, j = domain * BLOCKS + first, other * BLOCKS + second
        return i, j, jnp.where(live, i, spare), jnp.where(live, j, spare), apart

    def work(base, count):
        found = [find(base + index) for index in range(count)]
        for index, (i, j, _, _, apart) in enumerate(found):
            parts = weights(offsets_of(offsets, i), offsets_of(offsets, j), apart)
            high[index], low[index] = parts
        for index, (i, j, to_i, to_j, apart) in enumerate(found):
            x, y = offsets_of(offsets, i), offsets_of(offsets, j)
            xs = [x[c] + apart[c] for c in range(3)]
            ys = [y[c] - apart[c] for c in range(3)]
            on_i = apply(rows_of(moments, tile(j)), y, high[index], low[index], NT)
            on_j = apply(rows_of(moments, tile(i)), x, high[index], low[index], NN)
            for to, value in ((to_i, contract(on_i, xs)), (to_j, contract(on_j, ys))):
                stress[0, tile(to), :] += value[:, :LANES]
                stress[1, tile(to), :] += value[:, LANES:]

    whole, rest = total >> 3, total & 7
    rounds = whole + (rest > FEW).astype(I32)

    def many(turn, carry):
        work(turn * MANY, MANY)
        return carry

    def few(turn, carry):
        work(whole * MANY, FEW)
        return carry

    lax.fori_loop(0, rounds, many, 0)
    lax.fori_loop(0, ((rest > 0) & (rest <= FEW)).astype(I32), few, 0)


def pair_kernel(groups, parts, ints, *refs):
    states = refs[:parts]
    stress, moments, offsets, high, low, todo = refs[parts:]
    fill(states, moments, offsets)
    stress[...] = jnp.zeros_like(stress)
    all_pairs(ints, groups, todo, moments, offsets, stress, high, low)


def beyond_kernel(beyond, crossing, sources, out):
    finish(beyond, [(crossing, 4)], far_field(sources[...]), 4, out)


def near_kernel(near, inner, crossing, sources, out):
    finish(near, [(inner, 0), (crossing, 0)], far_field(sources[...]), 0, out)


def far_field(sources):
    row, lane = iota((64, LANES), 0), iota((64, LANES), 1)
    steps = []
    for member, size in enumerate((4, 4, 8)):
        place = 2 * ((lane >> (4, 5, 3)[member]) & 1)
        if member == 2:
            place = place + 4 * ((lane >> 6) & 1)
        step = place - ((row >> (3 + member)) & 1)
        steps.append(jnp.where(step > size // 2, step - size, step))
    most = functools.reduce(jnp.maximum, [jnp.abs(s) for s in steps])
    mask = (most > 1).astype(F32)
    tree = sources[6:7]
    r = []
    for member in range(3):
        bit = 2 - member
        at = 0.25 + 0.5 * ((row >> bit) & 1).astype(F32)
        own = 0.25 + 0.5 * ((lane >> bit) & 1).astype(F32)
        r.append(at - (jnp.where(tree == 1.0, own, 0.5) + steps[member].astype(F32)))
    xx, yy, zz, yz, xz, xy = [sources[m : m + 1] * mask for m in range(6)]
    inverse = lax.rsqrt(r[0] * r[0] + r[1] * r[1] + r[2] * r[2] + CORE)
    cubed = inverse * inverse * inverse
    weight = 3.0 * cubed * inverse * inverse
    ax = xx * r[0] + xy * r[1] + xz * r[2]
    ay = xy * r[0] + yy * r[1] + yz * r[2]
    az = xz * r[0] + yz * r[1] + zz * r[2]
    stress = [
        xx * cubed - weight * ax * r[0],
        yy * cubed - weight * ay * r[1],
        zz * cubed - weight * az * r[2],
        yz * cubed - 0.5 * weight * (ay * r[2] + az * r[1]),
        xz * cubed - 0.5 * weight * (ax * r[2] + az * r[0]),
        xy * cubed - 0.5 * weight * (ax * r[1] + ay * r[0]),
    ]
    out = []
    for value in stress:
        total = jnp.sum(value, axis=1, keepdims=True)
        out.append(jnp.sum(jnp.where(row == lane, total, 0.0), axis=0, keepdims=True))
    return out


def in_vmem(count):
    return [pl.BlockSpec(memory_space=pltpu.VMEM)] * count


def in_smem(count):
    return [pl.BlockSpec(memory_space=pltpu.SMEM)] * count


PARAMS = pltpu.CompilerParams(vmem_limit_bytes=VMEM_LIMIT)


def make_message(count, raw, notes):
    return pl.pallas_call(
        message_kernel,
        out_shape=jax.ShapeDtypeStruct((ROWS, LANES), F32),
        in_specs=in_smem(1) + in_vmem(2),
        out_specs=in_vmem(1)[0],
        compiler_params=PARAMS,
    )(count, raw, notes)


def make_source(tree, message):
    return pl.pallas_call(
        source_kernel,
        out_shape=jax.ShapeDtypeStruct((8, LANES), F32),
        in_specs=in_smem(1) + in_vmem(1),
        out_specs=in_vmem(1)[0],
        compiler_params=PARAMS,
    )(tree, message)


FORCES = jax.ShapeDtypeStruct((4 * PART, LANES), F32)
WORK = [pltpu.VMEM((MANY, WIDTH, WIDTH), BF16)] * 2 + [pltpu.SMEM((8 * CAP + 8,), I32)]


def pair_stress(groups, states):
    ints = [v.reshape(4, ROWS, LANES)[:, STATE:].reshape(-1, LANES) for v in states]
    blocks = 4 * len(states) * BLOCKS
    tiles = pltpu.VMEM((2, blocks * 8, LANES), F32)
    return pl.pallas_call(
        functools.partial(pair_kernel, groups, len(states)),
        out_shape=jax.ShapeDtypeStruct((2, (blocks + 1) * 8, LANES), F32),
        in_specs=in_smem(1) + in_vmem(len(states)),
        out_specs=in_vmem(1)[0],
        scratch_shapes=[tiles, tiles] + WORK,
        compiler_params=PARAMS,
        cost_estimate=pl.CostEstimate(flops=10**9, bytes_accessed=10**6, transcendentals=10**6),
    )(jnp.concatenate(ints).astype(I32), *states)


def forces(kernel, *arrays):
    return pl.pallas_call(
        kernel,
        out_shape=FORCES,
        in_specs=in_vmem(len(arrays)),
        out_specs=in_vmem(1)[0],
        compiler_params=PARAMS,
    )(*arrays)


def from_ahead(x, axis, by):
    size = lax.axis_size(axis)
    return lax.ppermute(x, axis, [(i, (i - by) % size) for i in range(size)])


def to_ahead(x, axis):
    size = lax.axis_size(axis)
    return lax.ppermute(x, axis, [(i, (i + 1) % size) for i in range(size)])


def grown(sources, axis, by):
    return jnp.concatenate([sources, from_ahead(sources, axis, by)], axis=1)


def shards(offsets, burgers, segvec, block_cell, tree_level, pair_count, pair_list):
    raw = jnp.concatenate([v.reshape(PART, LANES) for v in (offsets, burgers, segvec)])
    notes = [
        jnp.pad(pair_list.reshape(3, CAP), ((0, 0), (0, LANES - CAP))),
        jnp.pad(block_cell.reshape(1, BLOCKS), ((0, 0), (0, LANES - BLOCKS))),
    ]
    message = make_message(pair_count, raw, jnp.concatenate(notes))
    sources = make_source(tree_level, message)[:, :8]
    ahead = from_ahead(message, "gx", 1)
    sources = grown(sources, "gz", 2)
    line = jnp.concatenate([message, ahead])
    ahead = from_ahead(line, "gy", 1)
    ahead, sources = lax.optimization_barrier((ahead, grown(sources, "gx", 2)))
    near = jnp.concatenate([line, ahead])
    beyond = from_ahead(near, "gz", 1)
    inner = pair_stress([(d, d) for d in range(4)], [near])
    sources = grown(sources, "gy", 2)
    beyond, inner, sources = lax.optimization_barrier((beyond, inner, sources))
    groups = [(4 + d, d) for d in range(4)] + [(8 + d, 4 + d) for d in range(4)]
    crossing = pair_stress(groups, [near, beyond])
    sources = grown(sources, "gz", 4)
    force = to_ahead(forces(beyond_kernel, beyond, crossing, sources), "gz")
    force = force + forces(near_kernel, near, inner, crossing, sources)
    force = force[: 2 * PART] + to_ahead(force[2 * PART :], "gy")
    force = force[:PART] + to_ahead(force[PART:], "gx")
    return force.reshape(offsets.shape)


def solution(mesh):
    in_specs = (
        P("gx", "gy", "gz", None, None),
        P("gx", "gy", "gz", None, None),
        P("gx", "gy", "gz", None, None),
        P("gx", "gy", "gz", None),
        P(("gx", "gy", "gz")),
        P(("gx", "gy", "gz")),
        P("gx", "gy", "gz", None, None),
    )
    out_specs = P("gx", "gy", "gz", None, None)
    return jax.shard_map(shards, mesh=mesh, in_specs=in_specs, out_specs=out_specs, check_vma=False)
```
